256 devices in a mesh: tok: 16 (over x_lo, y, core), voc: 16 (over x_hi, z).
Axes of the slice: x: 4 (x_hi: 2, x_lo: 2; x = x_hi * 2 + x_lo), y: 4, z: 8, core: 2. Of those that a mesh axis runs over, the one named last changes fastest.
Arguments:
- resid: bfloat16 [512, 3584], P('tok'), may hold values from -50 to 50
- norm_gain: float32 [3584], replicated, may hold values from 0.5 to 1.5
- unembed: bfloat16 [3584, 196608], P(None, ('tok', 'voc')), may hold values from -0.7349684 to 0.7349684
- targets: int32 [512], replicated, may hold values from 0 to 196607
- feat_ids: int32 [512, 64], P('tok'), may hold values from 0 to 16383, all different within a row
- feat_acts: float32 [512, 64], P('tok'), may hold values from 0.5 to 4
- decoder: bfloat16 [3584, 16384], P('voc'), may hold values from -1.796875 to 1.796875
Outputs:
- attribution: float32 [512, 64], P('tok')
The draws below stay inside these ranges and needn't reach their ends.
All inputs are finite; a program needn't handle non-finite values.
Results may differ from the reference program's by a relative error of at most 0.0029.
Values may be sent and summed in bfloat16 or wider, within the bound.
A program may use at most 128 MiB of HBM per device.

```python
import math
import jax
import jax.numpy as jnp
from jax import lax

D = 3584
F = 16384
VOC_DEV = 768
K = 64
TOK_DEV = 32
TOKENS = 512
V = 196608
N_TOK = 16
N_VOC = 16


STRENGTHS = (1.0, 1.2, 1.4, 1.6, 1.8, 2.0, 2.2, 2.4)


def shared_draw(key):
    raw_weight = jax.random.truncated_normal(key, -6.0, 6.0, (D, V), jnp.float32)
    pair_key = jax.random.fold_in(key, 101)
    first_cols = jax.random.randint(pair_key, (8,), 0, V)
    shift_cols = jax.random.randint(jax.random.fold_in(pair_key, 1), (8,), 1, V)
    second_cols = (first_cols + shift_cols) % V
    return (raw_weight, first_cols, second_cols)


def draw_unembed(key, part):
    raw_weight, first_cols, second_cols = shared_draw(key)
    strength = jnp.array(STRENGTHS, jnp.float32)
    column_scale = jnp.ones((V,), jnp.float32)
    column_scale = column_scale.at[first_cols].set(strength).at[second_cols].set(strength)
    return (raw_weight * (3.0 / math.sqrt(D)) * column_scale).astype(jnp.bfloat16)


def draw_resid(key, part):
    raw_weight, first_cols, second_cols = shared_draw(key)
    key = jax.random.fold_in(key, 5)
    values = jax.random.truncated_normal(key, -6.0, 6.0, (TOKENS, D), jnp.float32)
    picked_rows = jnp.arange(8, dtype=jnp.int32) * (TOKENS // 8)
    aligned = jnp.transpose(raw_weight[:, first_cols] + 0.98 * raw_weight[:, second_cols])
    values = values.at[picked_rows].set(aligned + 0.1 * values[picked_rows])
    return values.astype(jnp.bfloat16)


def plant(values, key, low, high):
    shape = values.shape
    place = [jax.random.randint(jax.random.fold_in(key, axis), (), 0, shape[axis]) for axis in range(len(shape))]
    values = values.at[tuple(place)].set(low)
    longest = shape.index(max(shape))
    place[longest] = (place[longest] + 1) % shape[longest]
    return values.at[tuple(place)].set(high)


def level_of(key, extent, shards, least, largest):
    gain = 1.0
    for position, blocks in shards:
        heights = jax.random.uniform(jax.random.fold_in(jax.random.fold_in(key, 6), position), (blocks,), jnp.float32, least / len(shards), largest / len(shards))
        gain = gain * jnp.repeat(jnp.exp(heights), extent[position] // blocks).reshape((-1,) + (1,) * (len(extent) - 1 - position))
    return gain


def different_ones(rng, rows, count, top, lift):
    ranking = jax.random.permutation(jax.random.fold_in(rng, 1), count)
    favour = ranking
    for power in range(3):
        favour = favour * favour // count
    favour = favour * lift // count
    lots = jax.random.randint(jax.random.fold_in(rng, 2), (rows, count), 0, 4096) + favour
    fixed_rows = jax.random.permutation(jax.random.fold_in(rng, 3), rows)[jnp.arange(count) % rows]
    lots = jnp.where(jnp.arange(rows)[:, None] == fixed_rows[None, :], 1 << 14, lots)
    priority = lots * count + jnp.arange(count)
    return lax.top_k(priority.astype(jnp.int32), top)[1].astype(jnp.int32)


def bell_draw(rng, dims, width, reach, split=(), held_as=jnp.bfloat16):
    values = width * jax.random.normal(rng, dims, jnp.float32)
    if split:
        values = values * level_of(rng, dims, split, -0.22, 0.18)
    return jnp.clip(values, -reach, reach).astype(held_as)


def setup_inputs(seed: int = 0) -> dict:
    arg_keys = jax.random.split(jax.random.key(seed), 8)
    resid = draw_resid(jax.random.fold_in(arg_keys[7], 71), 0)
    norm_gain = jnp.clip(1.0 + 0.1 * jax.random.normal(arg_keys[1], (D,), jnp.float32), 0.5, 1.5)
    unembed = draw_unembed(jax.random.fold_in(arg_keys[7], 71), 0)
    targets = plant(jax.random.randint(arg_keys[3], (TOKENS,), 0, V), jax.random.fold_in(arg_keys[3], 1), 0, V - 1).astype(jnp.int32)
    feat_ids = different_ones(arg_keys[4], TOKENS, F, K, 0)
    feat_acts = jnp.clip(0.5 + 3.5 * jax.random.uniform(arg_keys[5], (TOKENS, K), jnp.float32) ** level_of(arg_keys[5], (TOKENS, K), ((0, 16),), -0.2, 0.2), 0.5, 4.0)
    decoder = bell_draw(arg_keys[6], (D, F), 0.3, 1.796875, ((0, 16),))
    return {"resid": resid, "norm_gain": norm_gain, "unembed": unembed, "targets": targets, "feat_ids": feat_ids, "feat_acts": feat_acts, "decoder": decoder}


EPSILON = 1e-06

def reference(resid, norm_gain, unembed, targets, feat_ids, feat_acts, decoder):
    hidden = resid.astype(jnp.float32)
    row_rms = jnp.sqrt(lax.optimization_barrier(jnp.mean(hidden * hidden, axis=1)) + EPSILON)
    normed = (hidden / row_rms[:, None] * norm_gain).astype(jnp.bfloat16)
    block_cols = VOC_DEV * N_VOC
    starts = jnp.arange(V // block_cols, dtype=jnp.int32) * block_cols

    def gather_stats(running, block_start):
        softmax_top, softmax_sum = running
        weights = lax.dynamic_slice_in_dim(unembed, block_start, block_cols, 1)
        logits = jnp.dot(normed, weights, preferred_element_type=jnp.float32)
        merged_top = jnp.maximum(softmax_top, lax.optimization_barrier(jnp.max(logits, axis=1)))
        softmax_sum = softmax_sum * jnp.exp(softmax_top - merged_top) + lax.optimization_barrier(jnp.sum(jnp.exp(logits - merged_top[:, None]), axis=1))
        return ((merged_top, softmax_sum), None)
    initial = (jnp.full((TOKENS,), -jnp.inf, jnp.float32), jnp.zeros((TOKENS,), jnp.float32))
    (softmax_top, softmax_sum), unused = lax.scan(gather_stats, initial, starts)

    def gather_grad(running, block_start):
        weights = lax.dynamic_slice_in_dim(unembed, block_start, block_cols, 1)
        logits = jnp.dot(normed, weights, preferred_element_type=jnp.float32)
        columns = block_start + jnp.arange(block_cols, dtype=jnp.int32)
        onehot = (targets[:, None] == columns[None, :]).astype(jnp.float32)
        direction = (onehot - jnp.exp(logits - softmax_top[:, None]) / softmax_sum[:, None]).astype(jnp.bfloat16)
        return (running + jnp.dot(direction, weights.T, preferred_element_type=jnp.float32), None)
    grad_normed, unused = lax.scan(gather_grad, jnp.zeros((TOKENS, D), jnp.float32), starts)
    unit = hidden / row_rms[:, None]
    scaled = grad_normed * norm_gain
    inner_mean = lax.optimization_barrier(jnp.mean(unit * scaled, axis=1))
    grad_resid = (scaled - unit * inner_mean[:, None]) / row_rms[:, None]

    def attribute(token_block):
        row_ids, grads, activations = token_block
        decoder_cols = decoder[:, row_ids].astype(jnp.float32)
        return jnp.einsum('dtk,td->tk', decoder_cols, grads, precision=lax.Precision.HIGHEST) * activations
    blocks = (feat_ids.reshape(N_TOK, TOK_DEV, K), grad_resid.reshape(N_TOK, TOK_DEV, D), feat_acts.reshape(N_TOK, TOK_DEV, K))
    return lax.map(attribute, blocks).reshape(TOKENS, K)
```

```python
import functools

import jax
import jax.numpy as jnp
from jax import lax
from jax.experimental import pallas as pl
from jax.experimental.pallas import tpu as pltpu
from jax.sharding import PartitionSpec as P

EPSILON = 1e-06
MESH = pl.DeviceIdType.MESH
F32 = jnp.float32
BF16 = jnp.bfloat16


def body(
    resid_ref, gain_ref, unembed_hbm, rel_ref, ids_ref, acts_ref, decoder_hbm,
    out_ref,
    w_ref, dec_ref, nall, ebuf, dirbuf, rms_ref, uslab, gslab, idbuf,
    st_own, st_in, acc, crecv, sx, sy, rx, ry, s2x, s2y, r2x, r2y, zs, zr,
    bz, az, fx_own, fx_in,
    load_sem, gy_s, gy_r, gx_s, gx_r, gc_s, gc_r, gd_s, gd_r, st_s, st_r,
    c_s, c_r, x1_s, x1_r, y1_s, y1_r, x2_s, x2_r, y2_s, y2_r, z_s, z_r,
    bz_s, bz_r, az_s, az_r, fx_s, fx_r,
):
    tok = lax.axis_index("tok")
    voc = lax.axis_index("voc")
    x_lo = tok // 8
    y = (tok // 2) % 4
    core = tok % 2
    x_hi = voc // 8
    z = voc % 8
    x = x_hi * 2 + x_lo

    def device(xx, yy, zz, cc):
        return ((xx % 2) * 8 + yy * 2 + cc, (xx // 2) * 8 + zz)

    def x_peer(k):
        return device((x + k) % 4, y, z, core)

    def y_peer(k):
        return device(x, (y + k) % 4, z, core)

    def z_peer(k):
        return device(x, y, (z + k) % 8, core)

    sibling = device(x, y, z, 1 - core)

    def send(src, dst, s, r, peer):
        return pltpu.make_async_remote_copy(
            src_ref=src, dst_ref=dst, send_sem=s, recv_sem=r, device_id=peer, device_id_type=MESH
        )

    load_w = pltpu.make_async_copy(unembed_hbm, w_ref, load_sem.at[0])
    load_d = pltpu.make_async_copy(decoder_hbm, dec_ref, load_sem.at[1])
    load_w.start()
    load_d.start()
    barrier = pltpu.get_barrier_semaphore()
    peers = [sibling]
    peers += [x_peer(k) for k in (1, 2, 3)]
    peers += [y_peer(k) for k in (1, 2, 3)]
    peers += [z_peer(k) for k in range(1, 8)]
    for peer in peers:
        pl.semaphore_signal(barrier, inc=1, device_id=peer, device_id_type=MESH)

    hidden = resid_ref[...].astype(F32)
    width = hidden.shape[1]
    rms = jnp.sqrt(jnp.mean(hidden * hidden, axis=1, keepdims=True) + EPSILON)
    rms_ref[...] = jnp.broadcast_to(rms, rms_ref.shape)
    nall[x_lo, core, y] = (hidden / rms * gain_ref[...]).astype(BF16)

    half = width // 2
    slab = half // 8
    start = pl.multiple_of(x_hi * half, half)
    unit_half = resid_ref[:, pl.ds(start, half)].astype(F32) / rms
    gain_half = gain_ref[:, pl.ds(start, half)]
    for zz in range(8):
        @pl.when(z == zz)
        def _():
            uslab[...] = unit_half[:, zz * slab:(zz + 1) * slab]
            gslab[...] = gain_half[:, zz * slab:(zz + 1) * slab]
    idbuf[...] = jnp.zeros_like(idbuf)
    idbuf[:, 0:64] = ids_ref[...]

    pl.semaphore_wait(barrier, len(peers))

    def gy(k):
        part = nall.at[x_lo, core, y]
        return send(part, part, gy_s.at[k - 1], gy_r.at[k - 1], y_peer(k))

    def gx(kb, d):
        part = nall.at[x_lo, core, (y - kb + 4) % 4, pl.ds(16 * d, 16)]
        return send(part, part, gx_s.at[kb, d], gx_r.at[kb, d], x_peer(1 if d == 0 else 3))

    def gc(kb):
        part = nall.at[x_lo, core, (y - kb + 4) % 4]
        return send(part, part, gc_s.at[kb], gc_r.at[kb], sibling)

    def gd(kb):
        part = nall.at[1 - x_lo, core, (y - kb + 4) % 4]
        return send(part, part, gd_s.at[kb], gd_r.at[kb], sibling)

    for k in (1, 3, 2):
        gy(k).start()
    gx(0, 0).start()
    gx(0, 1).start()
    gc(0).start()

    def attribute(values):
        high = values.astype(BF16)
        low = (values - high.astype(F32)).astype(BF16)
        stacked = jnp.concatenate([high, low], axis=0)
        lanes = jnp.bitwise_and(idbuf[...], 127)
        tiles = jnp.right_shift(idbuf[...], 7)

        def step(n, picked):
            cols = pl.ds(pl.multiple_of(n * 1024, 1024), 1024)
            both = jnp.dot(stacked, dec_ref[:, cols], preferred_element_type=F32)
            dots = both[0:32] + both[32:64]
            for q in range(8):
                got = jnp.take_along_axis(
                    dots[:, q * 128:(q + 1) * 128], lanes, axis=1, mode="promise_in_bounds"
                )
                picked = jnp.where(tiles == n * 8 + q, got, picked)
            return picked

        return lax.fori_loop(0, dec_ref.shape[1] // 1024, step, jnp.zeros((32, 128), F32))

    def to_voc(buf, s, r):
        return [send(buf.at[z], buf.at[z], s.at[k - 1], r.at[k - 1], z_peer(k)) for k in range(1, 8)]

    load_d.wait()
    bz[z] = attribute(uslab[...])
    for copy in to_voc(bz, bz_s, bz_r):
        copy.start()

    for k in (1, 3, 2):
        gy(k).wait_recv()
        gx(k, 0).start()
        gx(k, 1).start()
        gc(k).start()

    load_w.wait()

    eye = lax.broadcasted_iota(jnp.int32, (128, 128), 0) == lax.broadcasted_iota(jnp.int32, (128, 128), 1)

    def to_row(col):
        return jnp.sum(jnp.where(eye, col, 0.0), axis=0, keepdims=True)

    def to_col(row):
        return jnp.sum(jnp.where(eye, row, 0.0), axis=1, keepdims=True)

    def logits_of(xl):
        def step(n, carry):
            cols = pl.ds(pl.multiple_of(n * 256, 256), 256)
            left = nall[xl].reshape(256, width)
            ebuf[xl, :, cols] = jnp.dot(left, w_ref[:, cols], preferred_element_type=F32)
            return carry

        lax.fori_loop(0, ebuf.shape[2] // 256, step, 0)
        for q in range(2):
            rows = pl.ds(q * 128, 128)
            part = ebuf[xl, rows]
            top = jnp.max(part, axis=1, keepdims=True)
            part = jnp.exp(part - top)
            ebuf[xl, rows] = part
            st_own[0, pl.ds(xl * 2 + q, 1)] = to_row(top)
            st_own[0, pl.ds(4 + xl * 2 + q, 1)] = to_row(jnp.sum(part, axis=1, keepdims=True))

    for k in (0, 1, 3, 2):
        gc(k).wait_recv()
    logits_of(x_lo)
    for k in (0, 1, 3, 2):
        gx(k, 0).wait_recv()
        gx(k, 1).wait_recv()
        gd(k).start()
    for k in (0, 1, 3, 2):
        gd(k).wait_recv()
    logits_of(1 - x_lo)

    own = st_own[0]
    top, total = own[0:4], own[4:8]
    first_top = top
    groups = [peers[0:1], peers[1:4], peers[4:7], peers[7:14]]
    index = 0
    for stage, group in enumerate(groups):
        if stage > 0:
            st_own[stage, 0:4] = top
            st_own[stage, 4:8] = total
        copies = []
        for peer in group:
            copies.append(send(st_own.at[stage], st_in.at[index], st_s.at[index], st_r.at[index], peer))
            copies[-1].start()
            index += 1
        tiles = [(top, total)]
        for n, copy in enumerate(copies):
            copy.wait_recv()
            got = st_in[index - len(copies) + n]
            tiles.append((got[0:4], got[4:8]))
        merged = functools.reduce(jnp.maximum, [t for t, _ in tiles])
        total = sum(s * jnp.exp(t - merged) for t, s in tiles)
        top = merged
    scale = jnp.exp(first_top - top) / total
    voc_cols = w_ref.shape[1]
    lane = lax.broadcasted_iota(jnp.int32, (128, voc_cols), 1).astype(F32)
    for q in range(4):
        prob = ebuf[q // 2, pl.ds((q % 2) * 128, 128)] * to_col(scale[q:q + 1])
        hot = jnp.where(lane == to_col(rel_ref[q:q + 1, :]), 1.0, 0.0)
        dirbuf[pl.ds(q * 128, 128)] = (hot - prob).astype(BF16)

    def c_copy(j):
        return send(acc.at[1 - core, j], crecv.at[j], c_s.at[j], c_r.at[j], sibling)

    def x1(j, k):
        to = (x + k) % 4
        return send(sx.at[j, to // 2, to % 2], rx.at[j, k - 1], x1_s.at[j, k - 1], x1_r.at[j, k - 1], x_peer(k))

    def y1(j, k):
        return send(sy.at[j, (y + k) % 4], ry.at[j, k - 1], y1_s.at[j, k - 1], y1_r.at[j, k - 1], y_peer(k))

    def x2(j, k):
        to = (x + k) % 4
        return send(s2x.at[j, to // 2, to % 2], r2x.at[j, k - 1], x2_s.at[j, k - 1], x2_r.at[j, k - 1], x_peer(k))

    def y2(j, k):
        return send(s2y.at[j, (y + k) % 4], r2y.at[j, k - 1], y2_s.at[j, k - 1], y2_r.at[j, k - 1], y_peer(k))

    def z3(j):
        return send(zs.at[j], zr.at[j], z_s.at[j], z_r.at[j], z_peer(j + 1))

    def pipeline(i, carry):
        @pl.when(i < 8)
        def _():
            group = (z + 1 + i) % 8
            for hx in range(2):
                rows = pl.ds(pl.multiple_of(hx * half + group * slab, 32), slab)
                part = lax.dot_general(
                    dirbuf[...], w_ref[rows, :], (((1,), (1,)), ((), ())), preferred_element_type=F32
                )
                for q in range(4):
                    acc[q % 2, i, hx, q // 2] = part[q * 128:(q + 1) * 128].reshape(4, 32, slab)
            c_copy(i).start()

        @pl.when((i >= 1) & (i < 9))
        def _():
            j = i - 1
            c_copy(j).wait_recv()
            for hx in range(2):
                for xl in range(2):
                    both = acc[core, j, hx, xl] + crecv[j, hx, xl]
                    acc[core, j, hx, xl] = both
                    sx[j, hx, xl] = both[:, 0:16].astype(BF16)
                    for yy in range(4):
                        sy[j, yy, hx, xl] = both[yy, 16:32].astype(BF16)
            for k in (2, 1, 3):
                x1(j, k).start()
                y1(j, k).start()

        @pl.when((i >= 3) & (i < 11))
        def _():
            j = i - 3
            for k in (1, 2, 3):
                x1(j, k).wait_recv()
            mine = acc[core, j, x_hi, x_lo, :, 0:16]
            for k in range(3):
                mine = mine + rx[j, k].astype(F32)
            s2y[j] = mine
            for k in (2, 1, 3):
                y2(j, k).start()
            for k in (1, 2, 3):
                y1(j, k).wait_recv()
            other = acc[core, j, :, :, y, 16:32]
            for k in range(3):
                other = other + ry[j, k].astype(F32)
            s2x[j] = other
            for k in (2, 1, 3):
                x2(j, k).start()

        @pl.when(i >= 5)
        def _():
            j = i - 5
            for k in (1, 2, 3):
                y2(j, k).wait_recv()
            upper = s2y[j, y]
            for k in range(3):
                upper = upper + r2y[j, k]
            zs[j, 0:16] = upper
            for k in (1, 2, 3):
                x2(j, k).wait_recv()
            lower = s2x[j, x_hi, x_lo]
            for k in range(3):
                lower = lower + r2x[j, k]
            zs[j, 16:32] = lower

            @pl.when(j < 7)
            def _():
                z3(j).start()

        return carry

    lax.fori_loop(0, 13, pipeline, 0)
    grad = zs[7]
    for j in range(7):
        z3(j).wait_recv()
        grad = grad + zr[j]

    scaled = grad * gslab[...]
    inner = jnp.sum(uslab[...] * scaled, axis=1, keepdims=True)
    picked = attribute(scaled)
    lane = lax.broadcasted_iota(jnp.int32, (32, 128), 1)
    az[z] = jnp.where(lane < 64, picked, inner)
    for copy in to_voc(az, az_s, az_r):
        copy.start()
    for copy in to_voc(bz, bz_s, bz_r):
        copy.wait_recv()
    for copy in to_voc(az, az_s, az_r):
        copy.wait_recv()
    fx_own[0] = sum(az[n] for n in range(8))
    fx_own[1] = sum(bz[n] for n in range(8))
    last = send(fx_own, fx_in, fx_s.at[0], fx_r.at[0], x_peer(2))
    last.start()
    last.wait_recv()
    both = fx_own[0] + fx_in[0]
    unit_dot = fx_own[1] + fx_in[1]
    mean = both[:, 64:65] * (1.0 / width)
    out_ref[...] = ((both - unit_dot * mean) / rms_ref[...])[:, 0:64] * acts_ref[...]

    for k in (1, 2, 3):
        gy(k).wait_send()
    for k in range(4):
        gx(k, 0).wait_send()
        gx(k, 1).wait_send()
        gc(k).wait_send()
        gd(k).wait_send()
    index = 0
    for stage, group in enumerate(groups):
        for peer in group:
            send(st_own.at[stage], st_in.at[index], st_s.at[index], st_r.at[index], peer).wait_send()
            index += 1

    def drain(j, carry):
        c_copy(j).wait_send()
        for k in (1, 2, 3):
            x1(j, k).wait_send()
            y1(j, k).wait_send()
            x2(j, k).wait_send()
            y2(j, k).wait_send()

        @pl.when(j < 7)
        def _():
            z3(j).wait_send()

        return carry

    lax.fori_loop(0, 8, drain, 0)
    for copy in to_voc(bz, bz_s, bz_r) + to_voc(az, az_s, az_r):
        copy.wait_send()
    last.wait_send()


def on_device(resid, norm_gain, unembed, targets, feat_ids, feat_acts, decoder):
    width = resid.shape[1]
    voc_cols = unembed.shape[1]
    slab, features = decoder.shape
    block_index = lax.axis_index("tok") * 16 + lax.axis_index("voc")
    rel = (targets - block_index * voc_cols).astype(F32)
    rel = rel.reshape(2, 4, 2, 32).transpose(0, 2, 1, 3).reshape(4, 128)
    vm = pl.BlockSpec(memory_space=pltpu.VMEM)
    hbm = pl.BlockSpec(memory_space=pl.ANY)
    dma = pltpu.SemaphoreType.DMA
    return pl.pallas_call(
        body,
        out_shape=jax.ShapeDtypeStruct(feat_acts.shape, F32),
        in_specs=[vm, vm, hbm, vm, vm, vm, hbm],
        out_specs=vm,
        scratch_shapes=[
            pltpu.VMEM(unembed.shape, BF16),
            pltpu.VMEM(decoder.shape, BF16),
            pltpu.VMEM((2, 2, 4, 32, width), BF16),
            pltpu.VMEM((2, 256, voc_cols), F32),
            pltpu.VMEM((512, voc_cols), BF16),
            pltpu.VMEM((32, 128), F32),
            pltpu.VMEM((32, slab), F32),
            pltpu.VMEM((1, slab), F32),
            pltpu.VMEM((32, 128), jnp.int32),
            pltpu.VMEM((4, 8, 128), F32),
            pltpu.VMEM((14, 8, 128), F32),
            pltpu.VMEM((2, 8, 2, 2, 4, 32, slab), F32),
            pltpu.VMEM((8, 2, 2, 4, 32, slab), F32),
            pltpu.VMEM((8, 2, 2, 4, 16, slab), BF16),
            pltpu.VMEM((8, 4, 2, 2, 16, slab), BF16),
            pltpu.VMEM((8, 3, 4, 16, slab), BF16),
            pltpu.VMEM((8, 3, 2, 2, 16, slab), BF16),
            pltpu.VMEM((8, 2, 2, 16, slab), F32),
            pltpu.VMEM((8, 4, 16, slab), F32),
            pltpu.VMEM((8, 3, 16, slab), F32),
            pltpu.VMEM((8, 3, 16, slab), F32),
            pltpu.VMEM((8, 32, slab), F32),
            pltpu.VMEM((7, 32, slab), F32),
            pltpu.VMEM((8, 32, 128), F32),
            pltpu.VMEM((8, 32, 128), F32),
            pltpu.VMEM((2, 32, 128), F32),
            pltpu.VMEM((2, 32, 128), F32),
            dma((2,)),
            dma((3,)), dma((3,)),
            dma((4, 2)), dma((4, 2)),
            dma((4,)), dma((4,)),
            dma((4,)), dma((4,)),
            dma((14,)), dma((14,)),
            dma((8,)), dma((8,)),
            dma((8, 3)), dma((8, 3)),
            dma((8, 3)), dma((8, 3)),
            dma((8, 3)), dma((8, 3)),
            dma((8, 3)), dma((8, 3)),
            dma((7,)), dma((7,)),
            dma((7,)), dma((7,)),
            dma((7,)), dma((7,)),
            dma((1,)), dma((1,)),
        ],
        compiler_params=pltpu.CompilerParams(
            collective_id=0, has_side_effects=True, vmem_limit_bytes=60 * 1024 * 1024
        ),
    )(resid, norm_gain.reshape(1, width), unembed, rel, feat_ids, feat_acts, decoder)


def solution(mesh):
    placed = (
        P("tok", None),
        P(),
        P(None, ("tok", "voc")),
        P(),
        P("tok", None),
        P("tok", None),
        P("voc", None),
    )
    return jax.shard_map(
        on_device, mesh=mesh, in_specs=placed, out_specs=P("tok", None), check_vma=False
    )
```

```python
import functools

import jax
import jax.numpy as jnp
from jax import lax
from jax.experimental import pallas as pl
from jax.experimental.pallas import tpu as pltpu
from jax.sharding import PartitionSpec as P

EPSILON = 1e-06
MESH = pl.DeviceIdType.MESH
F32 = jnp.float32
BF16 = jnp.bfloat16


def body(
    resid_ref, gain_ref, unembed_hbm, targets_ref, ids_ref, decoder_hbm,
    out_ref,
    w_ref, dec_ref, nall, ebuf, dirbuf, rms_ref, gain_buf, uslab, gslab, idbuf,
    st_own, st_in, acc, crecv, sx, sy, rx, ry, s2x, s2y, r2x, r2y, zs, zr,
    bz, az, iz, bx, ax, ix,
    load_sem, gy_s, gy_r, gx_s, gx_r, gc_s, gc_r, gd_s, gd_r, st_s, st_r,
    c_s, c_r, x1_s, x1_r, y1_s, y1_r, x2_s, x2_r, y2_s, y2_r, z_s, z_r,
    bz_s, bz_r, az_s, az_r, iz_s, iz_r, fx_s, fx_r,
):
    tok = lax.axis_index("tok")
    voc = lax.axis_index("voc")
    x_lo = tok // 8
    y = (tok // 2) % 4
    core = tok % 2
    x_hi = voc // 8
    z = voc % 8
    x = x_hi * 2 + x_lo

    def device(xx, yy, zz, cc):
        return ((xx % 2) * 8 + yy * 2 + cc, (xx // 2) * 8 + zz)

    def x_peer(k):
        return device((x + k) % 4, y, z, core)

    def y_peer(k):
        return device(x, (y + k) % 4, z, core)

    def z_peer(k):
        return device(x, y, (z + k) % 8, core)

    sibling = device(x, y, z, 1 - core)

    def send(src, dst, s, r, peer):
        return pltpu.make_async_remote_copy(
            src_ref=src, dst_ref=dst, send_sem=s, recv_sem=r, device_id=peer, device_id_type=MESH
        )

    load_w = pltpu.make_async_copy(unembed_hbm, w_ref, load_sem.at[0])
    load_d = pltpu.make_async_copy(decoder_hbm, dec_ref, load_sem.at[1])
    load_w.start()
    load_d.start()
    barrier = pltpu.get_barrier_semaphore()
    peers = [sibling]
    peers += [x_peer(k) for k in (1, 2, 3)]
    peers += [y_peer(k) for k in (1, 2, 3)]
    peers += [z_peer(k) for k in range(1, 8)]
    for peer in peers:
        pl.semaphore_signal(barrier, inc=1, device_id=peer, device_id_type=MESH)

    hidden = resid_ref[...].astype(F32)
    width = hidden.shape[1]
    rms = jnp.sqrt(jnp.mean(hidden * hidden, axis=1, keepdims=True) + EPSILON)
    rms_ref[...] = jnp.broadcast_to(rms, rms_ref.shape)
    gain = gain_ref[...].reshape(1, width)
    gain_buf[...] = gain
    nall[x_lo, core, y] = (hidden / rms * gain).astype(BF16)

    half = width // 2
    slab = half // 8
    start = pl.multiple_of(x_hi * half, half)
    unit_half = resid_ref[:, pl.ds(start, half)].astype(F32) / rms
    gain_half = gain_buf[:, pl.ds(start, half)]
    for zz in range(8):
        @pl.when(z == zz)
        def _():
            uslab[...] = unit_half[:, zz * slab:(zz + 1) * slab]
            gslab[...] = gain_half[:, zz * slab:(zz + 1) * slab]
    idbuf[...] = jnp.zeros_like(idbuf)
    idbuf[:, 0:64] = ids_ref[...]

    pl.semaphore_wait(barrier, len(peers))

    def gy(k):
        part = nall.at[x_lo, core, y]
        return send(part, part, gy_s.at[k - 1], gy_r.at[k - 1], y_peer(k))

    def gx(kb, d):
        part = nall.at[x_lo, core, (y - kb + 4) % 4, pl.ds(16 * d, 16)]
        return send(part, part, gx_s.at[kb, d], gx_r.at[kb, d], x_peer(1 if d == 0 else 3))

    def gc(kb):
        part = nall.at[x_lo, core, (y - kb + 4) % 4]
        return send(part, part, gc_s.at[kb], gc_r.at[kb], sibling)

    def gd(kb):
        part = nall.at[1 - x_lo, core, (y - kb + 4) % 4]
        return send(part, part, gd_s.at[kb], gd_r.at[kb], sibling)

    for k in (1, 3, 2):
        gy(k).start()
    gx(0, 0).start()
    gx(0, 1).start()
    gc(0).start()

    low_half = lax.broadcasted_iota(jnp.int32, (16, 128), 1) < 64

    def attribute(values):
        high = values.astype(BF16)
        low = (values - high.astype(F32)).astype(BF16)
        stacked = jnp.concatenate([high, low], axis=0)
        lanes = jnp.bitwise_and(idbuf[...], 127)
        tiles = jnp.right_shift(idbuf[...], 7)

        def step(n, picked):
            cols = pl.ds(pl.multiple_of(n * 1024, 1024), 1024)
            both = jnp.dot(stacked, dec_ref[:, cols], preferred_element_type=F32)
            dots = both[0:32] + both[32:64]
            for q in range(8):
                got = jnp.take_along_axis(
                    dots[:, q * 128:(q + 1) * 128], lanes, axis=1, mode="promise_in_bounds"
                )
                picked = jnp.where(tiles == n * 8 + q, got, picked)
            return picked

        picked = lax.fori_loop(0, dec_ref.shape[1] // 1024, step, jnp.zeros((32, 128), F32))
        return jnp.where(low_half, picked[0:16], pltpu.roll(picked[16:32], 64, 1))

    def to_voc(buf, s, r):
        return [send(buf.at[z], buf.at[z], s.at[k - 1], r.at[k - 1], z_peer(k)) for k in range(1, 8)]

    load_d.wait()
    bz[z] = attribute(uslab[...])
    for copy in to_voc(bz, bz_s, bz_r):
        copy.start()

    for k in (1, 3, 2):
        gy(k).wait_recv()
        gx(k, 0).start()
        gx(k, 1).start()
        gc(k).start()

    load_w.wait()

    eye = lax.broadcasted_iota(jnp.int32, (128, 128), 0) == lax.broadcasted_iota(jnp.int32, (128, 128), 1)

    def to_row(col):
        return jnp.sum(jnp.where(eye, col, 0.0), axis=0, keepdims=True)

    def to_col(row):
        return jnp.sum(jnp.where(eye, row, 0.0), axis=1, keepdims=True)

    def logits_of(xl):
        def step(n, carry):
            cols = pl.ds(pl.multiple_of(n * 256, 256), 256)
            left = nall[xl].reshape(256, width)
            ebuf[xl, :, cols] = jnp.dot(left, w_ref[:, cols], preferred_element_type=F32)
            return carry

        lax.fori_loop(0, ebuf.shape[2] // 256, step, 0)
        for q in range(2):
            rows = pl.ds(q * 128, 128)
            part = ebuf[xl, rows]
            top = jnp.max(part, axis=1, keepdims=True)
            part = jnp.exp(part - top)
            ebuf[xl, rows] = part
            st_own[0, pl.ds(xl * 2 + q, 1)] = to_row(top)
            st_own[0, pl.ds(4 + xl * 2 + q, 1)] = to_row(jnp.sum(part, axis=1, keepdims=True))

    for k in (0, 1, 3, 2):
        gc(k).wait_recv()
    logits_of(x_lo)
    for k in (0, 1, 3, 2):
        gx(k, 0).wait_recv()
        gx(k, 1).wait_recv()
        gd(k).start()
    for k in (0, 1, 3, 2):
        gd(k).wait_recv()
    logits_of(1 - x_lo)

    own = st_own[0]
    top, total = own[0:4], own[4:8]
    first_top = top
    groups = [peers[0:1], peers[1:4], peers[4:7], peers[7:14]]
    index = 0
    for stage, group in enumerate(groups):
        if stage > 0:
            st_own[stage, 0:4] = top
            st_own[stage, 4:8] = total
        copies = []
        for peer in group:
            copies.append(send(st_own.at[stage], st_in.at[index], st_s.at[index], st_r.at[index], peer))
            copies[-1].start()
            index += 1
        tiles = [(top, total)]
        for n, copy in enumerate(copies):
            copy.wait_recv()
            got = st_in[index - len(copies) + n]
            tiles.append((got[0:4], got[4:8]))
        merged = functools.reduce(jnp.maximum, [t for t, _ in tiles])
        total = sum(s * jnp.exp(t - merged) for t, s in tiles)
        top = merged
    scale = jnp.exp(first_top - top) / total
    voc_cols = w_ref.shape[1]
    lane = lax.broadcasted_iota(jnp.int32, (128, voc_cols), 1).astype(F32)
    rel = (targets_ref[...] - (tok * 16 + voc) * voc_cols).astype(F32)
    cols = [to_col(rel[n:n + 1]) for n in range(4)]
    for q in range(4):
        prob = ebuf[q // 2, pl.ds((q % 2) * 128, 128)] * to_col(scale[q:q + 1])
        parts = []
        for yy in range(4):
            first = (yy % 2) * 64 + (q % 2) * 32
            parts.append(cols[(q // 2) * 2 + yy // 2][first:first + 32])
        hot = jnp.where(lane == jnp.concatenate(parts, axis=0), 1.0, 0.0)
        dirbuf[pl.ds(q * 128, 128)] = (hot - prob).astype(BF16)

    def cross(buf, n):
        return send(buf.at[0], buf.at[1], fx_s.at[n], fx_r.at[n], x_peer(2))

    def add_voc(buf, s, r, over, n):
        for copy in to_voc(buf, s, r):
            copy.wait_recv()
        over[0] = sum(buf[m] for m in range(8))
        cross(over, n).start()

    add_voc(bz, bz_s, bz_r, bx, 0)

    def c_copy(j):
        return send(acc.at[1 - core, j], crecv.at[j], c_s.at[j], c_r.at[j], sibling)

    def x1(j, k):
        to = (x + k) % 4
        return send(sx.at[j, to // 2, to % 2], rx.at[j, k - 1], x1_s.at[j, k - 1], x1_r.at[j, k - 1], x_peer(k))

    def y1(j, k):
        return send(sy.at[j, (y + k) % 4], ry.at[j, k - 1], y1_s.at[j, k - 1], y1_r.at[j, k - 1], y_peer(k))

    def x2(j, k):
        to = (x + k) % 4
        return send(s2x.at[j, to // 2, to % 2], r2x.at[j, k - 1], x2_s.at[j, k - 1], x2_r.at[j, k - 1], x_peer(k))

    def y2(j, k):
        return send(s2y.at[j, (y + k) % 4], r2y.at[j, k - 1], y2_s.at[j, k - 1], y2_r.at[j, k - 1], y_peer(k))

    def z3(j):
        return send(zs.at[j], zr.at[j], z_s.at[j], z_r.at[j], z_peer(j + 1))

    def pipeline(i, carry):
        @pl.when(i < 8)
        def _():
            group = (z + 1 + i) % 8
            for hx in range(2):
                rows = pl.ds(pl.multiple_of(hx * half + group * slab, 32), slab)
                part = lax.dot_general(
                    dirbuf[...], w_ref[rows, :], (((1,), (1,)), ((), ())), preferred_element_type=F32
                )
                for q in range(4):
                    acc[q % 2, i, hx, q // 2] = part[q * 128:(q + 1) * 128].reshape(4, 32, slab)
            c_copy(i).start()

        @pl.when((i >= 1) & (i < 9))
        def _():
            j = i - 1
            c_copy(j).wait_recv()
            for hx in range(2):
                for xl in range(2):
                    both = acc[core, j, hx, xl] + crecv[j, hx, xl]
                    acc[core, j, hx, xl] = both
                    sx[j, hx, xl] = both[:, 0:16].astype(BF16)
                    for yy in range(4):
                        sy[j, yy, hx, xl] = both[yy, 16:32].astype(BF16)
            for k in (2, 1, 3):
                x1(j, k).start()
                y1(j, k).start()

        @pl.when((i >= 3) & (i < 11))
        def _():
            j = i - 3
            for k in (1, 2, 3):
                x1(j, k).wait_recv()
            mine = acc[core, j, x_hi, x_lo, :, 0:16]
            for k in range(3):
                mine = mine + rx[j, k].astype(F32)
            acc[core, j, x_hi, x_lo, :, 0:16] = mine
            s2y[j] = mine.astype(BF16)
            for k in (2, 1, 3):
                y2(j, k).start()
            for k in (1, 2, 3):
                y1(j, k).wait_recv()
            other = acc[core, j, :, :, y, 16:32]
            for k in range(3):
                other = other + ry[j, k].astype(F32)
            acc[core, j, :, :, y, 16:32] = other
            s2x[j] = other.astype(BF16)
            for k in (2, 1, 3):
                x2(j, k).start()

        @pl.when(i >= 5)
        def _():
            j = i - 5
            for k in (1, 2, 3):
                y2(j, k).wait_recv()
            upper = acc[core, j, x_hi, x_lo, y, 0:16]
            for k in range(3):
                upper = upper + r2y[j, k].astype(F32)
            zs[j, 0:16] = upper
            for k in (1, 2, 3):
                x2(j, k).wait_recv()
            lower = acc[core, j, x_hi, x_lo, y, 16:32]
            for k in range(3):
                lower = lower + r2x[j, k].astype(F32)
            zs[j, 16:32] = lower

            @pl.when(j < 7)
            def _():
                z3(j).start()

        return carry

    lax.fori_loop(0, 13, pipeline, 0)
    grad = zs[7]
    for j in range(7):
        z3(j).wait_recv()
        grad = grad + zr[j]

    scaled = grad * gslab[...]
    inner = jnp.sum(uslab[...] * scaled, axis=1, keepdims=True)
    iz[z] = jnp.broadcast_to(inner, (32, 128))
    for copy in to_voc(iz, iz_s, iz_r):
        copy.start()
    az[z] = attribute(scaled)
    for copy in to_voc(az, az_s, az_r):
        copy.start()
    add_voc(iz, iz_s, iz_r, ix, 1)
    add_voc(az, az_s, az_r, ax, 2)
    cross(bx, 0).wait_recv()
    cross(ix, 1).wait_recv()
    unit_dot = bx[0] + bx[1]
    mean = (ix[0] + ix[1]) * (1.0 / width)
    scale = 1.0 / rms_ref[...]
    cross(ax, 2).wait_recv()
    both = ax[0] + ax[1]
    for n in range(2):
        rows = slice(n * 16, n * 16 + 16)
        if n == 1:
            both = pltpu.roll(both, 64, 1)
            unit_dot = pltpu.roll(unit_dot, 64, 1)
        out_ref[rows] = ((both - unit_dot * mean[rows]) * scale[rows])[:, 0:64]

    for k in (1, 2, 3):
        gy(k).wait_send()
    for k in range(4):
        gx(k, 0).wait_send()
        gx(k, 1).wait_send()
        gc(k).wait_send()
        gd(k).wait_send()
    index = 0
    for stage, group in enumerate(groups):
        for peer in group:
            send(st_own.at[stage], st_in.at[index], st_s.at[index], st_r.at[index], peer).wait_send()
            index += 1

    def drain(j, carry):
        c_copy(j).wait_send()
        for k in (1, 2, 3):
            x1(j, k).wait_send()
            y1(j, k).wait_send()
            x2(j, k).wait_send()
            y2(j, k).wait_send()

        @pl.when(j < 7)
        def _():
            z3(j).wait_send()

        return carry

    lax.fori_loop(0, 8, drain, 0)
    for copy in to_voc(bz, bz_s, bz_r) + to_voc(az, az_s, az_r) + to_voc(iz, iz_s, iz_r):
        copy.wait_send()
    for n, over in enumerate((bx, ix, ax)):
        cross(over, n).wait_send()


def on_device(resid, norm_gain, unembed, targets, feat_ids, feat_acts, decoder):
    width = resid.shape[1]
    voc_cols = unembed.shape[1]
    slab, features = decoder.shape
    vm = pl.BlockSpec(memory_space=pltpu.VMEM)
    hbm = pl.BlockSpec(memory_space=pl.ANY)
    dma = pltpu.SemaphoreType.DMA
    projected = pl.pallas_call(
        body,
        out_shape=jax.ShapeDtypeStruct(feat_acts.shape, F32),
        in_specs=[vm, vm, hbm, vm, vm, hbm],
        out_specs=vm,
        scratch_shapes=[
            pltpu.VMEM(unembed.shape, BF16),
            pltpu.VMEM(decoder.shape, BF16),
            pltpu.VMEM((2, 2, 4, 32, width), BF16),
            pltpu.VMEM((2, 256, voc_cols), F32),
            pltpu.VMEM((512, voc_cols), BF16),
            pltpu.VMEM((32, 128), F32),
            pltpu.VMEM((1, width), F32),
            pltpu.VMEM((32, slab), F32),
            pltpu.VMEM((1, slab), F32),
            pltpu.VMEM((32, 128), jnp.int32),
            pltpu.VMEM((4, 8, 128), F32),
            pltpu.VMEM((14, 8, 128), F32),
            pltpu.VMEM((2, 8, 2, 2, 4, 32, slab), F32),
            pltpu.VMEM((8, 2, 2, 4, 32, slab), F32),
            pltpu.VMEM((8, 2, 2, 4, 16, slab), BF16),
            pltpu.VMEM((8, 4, 2, 2, 16, slab), BF16),
            pltpu.VMEM((8, 3, 4, 16, slab), BF16),
            pltpu.VMEM((8, 3, 2, 2, 16, slab), BF16),
            pltpu.VMEM((8, 2, 2, 16, slab), BF16),
            pltpu.VMEM((8, 4, 16, slab), BF16),
            pltpu.VMEM((8, 3, 16, slab), BF16),
            pltpu.VMEM((8, 3, 16, slab), BF16),
            pltpu.VMEM((8, 32, slab), F32),
            pltpu.VMEM((7, 32, slab), F32),
            pltpu.VMEM((8, 16, 128), F32),
            pltpu.VMEM((8, 16, 128), F32),
            pltpu.VMEM((8, 32, 128), F32),
            pltpu.VMEM((2, 16, 128), F32),
            pltpu.VMEM((2, 16, 128), F32),
            pltpu.VMEM((2, 32, 128), F32),
            dma((2,)),
            dma((3,)), dma((3,)),
            dma((4, 2)), dma((4, 2)),
            dma((4,)), dma((4,)),
            dma((4,)), dma((4,)),
            dma((14,)), dma((14,)),
            dma((8,)), dma((8,)),
            dma((8, 3)), dma((8, 3)),
            dma((8, 3)), dma((8, 3)),
            dma((8, 3)), dma((8, 3)),
            dma((8, 3)), dma((8, 3)),
            dma((7,)), dma((7,)),
            dma((7,)), dma((7,)),
            dma((7,)), dma((7,)),
            dma((7,)), dma((7,)),
            dma((3,)), dma((3,)),
        ],
        compiler_params=pltpu.CompilerParams(
            collective_id=0, has_side_effects=True, vmem_limit_bytes=60 * 1024 * 1024
        ),
    )(resid, norm_gain, unembed, targets.reshape(4, 128), feat_ids, decoder)
    return projected * feat_acts


def solution(mesh):
    placed = (
        P("tok", None),
        P(),
        P(None, ("tok", "voc")),
        P(),
        P("tok", None),
        P("tok", None),
        P("voc", None),
    )
    return jax.shard_map(
        on_device, mesh=mesh, in_specs=placed, out_specs=P("tok", None), check_vma=False
    )
```

```python
import functools

import jax
import jax.numpy as jnp
from jax import lax
from jax.experimental import pallas as pl
from jax.experimental.pallas import tpu as pltpu
from jax.sharding import PartitionSpec as P

EPSILON = 1e-06
MESH = pl.DeviceIdType.MESH
F32 = jnp.float32
BF16 = jnp.bfloat16


def body(
    resid_ref, gain_ref, unembed_hbm, targets_ref, ids_ref, decoder_hbm,
    out_ref,
    w_ref, dec_ref, nall, ebuf, dirbuf, rms_ref, gain_buf, uslab, gslab, idbuf,
    st_own, st_in, acc, crecv, sx, sy, rx, ry, s2x, s2y, r2x, r2y, zs, zr,
    bz, az, iz, bx, ax, ix,
    load_sem, gy_s, gy_r, gx_s, gx_r, gc_s, gc_r, gd_s, gd_r, st_s, st_r,
    c_s, c_r, x1_s, x1_r, y1_s, y1_r, x2_s, x2_r, y2_s, y2_r, z_s, z_r,
    bz_s, bz_r, az_s, az_r, iz_s, iz_r, fx_s, fx_r,
):
    tok = lax.axis_index("tok")
    voc = lax.axis_index("voc")
    x_lo = tok // 8
    y = (tok // 2) % 4
    core = tok % 2
    x_hi = voc // 8
    z = voc % 8
    x = x_hi * 2 + x_lo

    def device(xx, yy, zz, cc):
        return ((xx % 2) * 8 + yy * 2 + cc, (xx // 2) * 8 + zz)

    def x_peer(k):
        return device((x + k) % 4, y, z, core)

    def y_peer(k):
        return device(x, (y + k) % 4, z, core)

    def z_peer(k):
        return device(x, y, (z + k) % 8, core)

    sibling = device(x, y, z, 1 - core)

    def send(src, dst, s, r, peer):
        return pltpu.make_async_remote_copy(
            src_ref=src, dst_ref=dst, send_sem=s, recv_sem=r, device_id=peer, device_id_type=MESH
        )

    load_w = pltpu.make_async_copy(unembed_hbm, w_ref, load_sem.at[0])
    load_d = pltpu.make_async_copy(decoder_hbm, dec_ref, load_sem.at[1])
    load_w.start()
    load_d.start()
    barrier = pltpu.get_barrier_semaphore()
    peers = [sibling]
    peers += [x_peer(k) for k in (1, 2, 3)]
    peers += [y_peer(k) for k in (1, 2, 3)]
    peers += [z_peer(k) for k in range(1, 8)]
    for peer in peers:
        pl.semaphore_signal(barrier, inc=1, device_id=peer, device_id_type=MESH)

    hidden = resid_ref[...].astype(F32)
    width = hidden.shape[1]
    rms = jnp.sqrt(jnp.mean(hidden * hidden, axis=1, keepdims=True) + EPSILON)
    rms_ref[...] = jnp.broadcast_to(rms, rms_ref.shape)
    gain = gain_ref[...].reshape(1, width)
    gain_buf[...] = gain
    normed = (hidden / rms * gain).astype(BF16)
    for h in range(2):
        nall[h, x_lo, core, y] = normed[h * 16:h * 16 + 16]

    half = width // 2
    slab = half // 8
    start = pl.multiple_of(x_hi * half, half)
    unit_half = resid_ref[:, pl.ds(start, half)].astype(F32) / rms
    gain_half = gain_buf[:, pl.ds(start, half)]
    for zz in range(8):
        @pl.when(z == zz)
        def _():
            uslab[...] = unit_half[:, zz * slab:(zz + 1) * slab]
            gslab[...] = gain_half[:, zz * slab:(zz + 1) * slab]
    st_own[...] = jnp.zeros_like(st_own)
    idbuf[...] = jnp.zeros_like(idbuf)
    idbuf[:, 0:64] = ids_ref[...]

    pl.semaphore_wait(barrier, len(peers))

    def gy(h, k):
        part = nall.at[h, x_lo, core, y]
        return send(part, part, gy_s.at[h, k - 1], gy_r.at[h, k - 1], y_peer(k))

    def gx(h, kb):
        part = nall.at[h, x_lo, core, (y - kb + 4) % 4]
        return send(part, part, gx_s.at[h, kb], gx_r.at[h, kb], x_peer(1 if kb % 2 == 0 else 3))

    def gc(h, kb):
        part = nall.at[h, x_lo, core, (y - kb + 4) % 4]
        return send(part, part, gc_s.at[h, kb], gc_r.at[h, kb], sibling)

    def gd(h, kb):
        part = nall.at[h, 1 - x_lo, core, (y - kb + 4) % 4]
        return send(part, part, gd_s.at[h, kb], gd_r.at[h, kb], sibling)

    def pass_on(h, k):
        gy(h, k).wait_recv()
        gx(h, k).start()
        gc(h, k).start()

    def pass_over(h, kb):
        gx(h, kb).wait_recv()
        gd(h, kb).start()

    def gathered(h):
        for kb in (0, 1, 3, 2):
            gc(h, kb).wait_recv()
            gd(h, kb).wait_recv()

    for h in range(2):
        for k in (1, 3, 2):
            gy(h, k).start()
        gx(h, 0).start()
        gc(h, 0).start()

    low_half = lax.broadcasted_iota(jnp.int32, (16, 128), 1) < 64

    def attribute(values):
        high = values.astype(BF16)
        low = (values - high.astype(F32)).astype(BF16)
        stacked = jnp.concatenate([high, low], axis=0)
        lanes = jnp.bitwise_and(idbuf[...], 127)
        tiles = jnp.right_shift(idbuf[...], 7)

        def step(n, picked):
            cols = pl.ds(pl.multiple_of(n * 1024, 1024), 1024)
            both = jnp.dot(stacked, dec_ref[:, cols], preferred_element_type=F32)
            dots = both[0:32] + both[32:64]
            for q in range(8):
                got = jnp.take_along_axis(
                    dots[:, q * 128:(q + 1) * 128], lanes, axis=1, mode="promise_in_bounds"
                )
                picked = jnp.where(tiles == n * 8 + q, got, picked)
            return picked

        picked = lax.fori_loop(0, dec_ref.shape[1] // 1024, step, jnp.zeros((32, 128), F32))
        return jnp.where(low_half, picked[0:16], pltpu.roll(picked[16:32], 64, 1))

    def to_voc(buf, s, r):
        return [send(buf.at[z], buf.at[z], s.at[k - 1], r.at[k - 1], z_peer(k)) for k in range(1, 8)]

    load_d.wait()
    bz[z] = attribute(uslab[...])
    for copy in to_voc(bz, bz_s, bz_r):
        copy.start()

    eye = lax.broadcasted_iota(jnp.int32, (128, 128), 0) == lax.broadcasted_iota(jnp.int32, (128, 128), 1)

    def to_row(col):
        return jnp.sum(jnp.where(eye, col, 0.0), axis=0, keepdims=True)

    def to_col(row):
        return jnp.sum(jnp.where(eye, row, 0.0), axis=1, keepdims=True)

    def logits_of(h):
        def step(n, carry):
            cols = pl.ds(pl.multiple_of(n * 256, 256), 256)
            left = nall[h].reshape(256, width)
            ebuf[h, :, cols] = jnp.dot(left, w_ref[:, cols], preferred_element_type=F32)
            return carry

        lax.fori_loop(0, ebuf.shape[2] // 256, step, 0)
        for q in range(2):
            rows = pl.ds(q * 128, 128)
            part = ebuf[h, rows]
            top = jnp.max(part, axis=1, keepdims=True)
            part = jnp.exp(part - top)
            ebuf[h, rows] = part
            st_own[h, 0, pl.ds(q, 1)] = to_row(top)
            st_own[h, 0, pl.ds(2 + q, 1)] = to_row(jnp.sum(part, axis=1, keepdims=True))

    firsts = [0, 1, 4, 7, 14]

    def st_copies(h, stage):
        return [
            send(st_own.at[h, stage], st_in.at[h, n], st_s.at[h, n], st_r.at[h, n], peers[n])
            for n in range(firsts[stage], firsts[stage + 1])
        ]

    def st_send(h, stage):
        for copy in st_copies(h, stage):
            copy.start()

    def st_merge(h, stage):
        for copy in st_copies(h, stage):
            copy.wait_recv()
        tiles = [st_own[h, stage]] + [st_in[h, n] for n in range(firsts[stage], firsts[stage + 1])]
        merged = functools.reduce(jnp.maximum, [t[0:2] for t in tiles])
        st_own[h, stage + 1, 0:2] = merged
        st_own[h, stage + 1, 2:4] = sum(t[2:4] * jnp.exp(t[0:2] - merged) for t in tiles)
        if stage < 3:
            st_send(h, stage + 1)

    voc_cols = w_ref.shape[1]

    def direction_of(h):
        scale = jnp.exp(st_own[h, 0, 0:2] - st_own[h, 4, 0:2]) / st_own[h, 4, 2:4]
        lane = lax.broadcasted_iota(jnp.int32, (128, voc_cols), 1).astype(F32)
        rel = (targets_ref[...] - (tok * 16 + voc) * voc_cols).astype(F32)
        cols = [to_col(rel[n:n + 1]) for n in range(4)]
        for q in range(2):
            prob = ebuf[h, pl.ds(q * 128, 128)] * to_col(scale[q:q + 1])
            parts = []
            for cc in range(2):
                for yy in range(4):
                    first = (yy % 2) * 64 + cc * 32 + h * 16
                    parts.append(cols[q * 2 + yy // 2][first:first + 16])
            hot = jnp.where(lane == jnp.concatenate(parts, axis=0), 1.0, 0.0)
            dirbuf[h, pl.ds(q * 128, 128)] = (hot - prob).astype(BF16)

    for k in (1, 3, 2):
        pass_on(0, k)
    for k in (1, 3):
        pass_on(1, k)
    for kb in (0, 1, 3, 2):
        pass_over(0, kb)
    pass_on(1, 2)
    load_w.wait()
    gathered(0)
    logits_of(0)
    st_send(0, 0)
    for kb in (0, 1, 3):
        pass_over(1, kb)
    st_merge(0, 0)
    pass_over(1, 2)
    gathered(1)
    logits_of(1)
    st_send(1, 0)
    st_merge(0, 1)
    st_merge(1, 0)
    st_merge(0, 2)
    st_merge(1, 1)

    def cross(buf, n):
        return send(buf.at[0], buf.at[1], fx_s.at[n], fx_r.at[n], x_peer(2))

    def add_voc(buf, s, r, over, n):
        for copy in to_voc(buf, s, r):
            copy.wait_recv()
        over[0] = sum(buf[m] for m in range(8))
        cross(over, n).start()

    add_voc(bz, bz_s, bz_r, bx, 0)
    st_merge(0, 3)
    direction_of(0)

    def c_copy(j):
        return send(acc.at[1 - core, j], crecv.at[j], c_s.at[j], c_r.at[j], sibling)

    def x1(j, k):
        to = (x + k) % 4
        return send(sx.at[j, to // 2, to % 2], rx.at[j, k - 1], x1_s.at[j, k - 1], x1_r.at[j, k - 1], x_peer(k))

    def y1(j, k):
        return send(sy.at[j, (y + k) % 4], ry.at[j, k - 1], y1_s.at[j, k - 1], y1_r.at[j, k - 1], y_peer(k))

    def x2(j, k):
        to = (x + k) % 4
        return send(s2x.at[j, to // 2, to % 2], r2x.at[j, k - 1], x2_s.at[j, k - 1], x2_r.at[j, k - 1], x_peer(k))

    def y2(j, k):
        return send(s2y.at[j, (y + k) % 4], r2y.at[j, k - 1], y2_s.at[j, k - 1], y2_r.at[j, k - 1], y_peer(k))

    def z3(j, sub):
        hop = 2 * (j % 4) + sub
        slot = (j // 4, hop)
        return send(zs.at[j, sub], zr.at[slot], z_s.at[slot], z_r.at[slot], z_peer(hop + 1))

    def multiply(j):
        for sub in range(2):
            group = (z + 1 + 2 * (j % 4) + sub) % 8
            for hx in range(2):
                rows = pl.ds(pl.multiple_of(hx * half + group * slab, 32), slab)
                part = lax.dot_general(
                    dirbuf[j // 4], w_ref[rows, :], (((1,), (1,)), ((), ())), preferred_element_type=F32
                )
                for q in range(4):
                    acc[q % 2, j, hx, q // 2, :, sub] = part[q * 64:(q + 1) * 64].reshape(4, 16, slab)
        c_copy(j).start()

    def first_sum(j):
        c_copy(j).wait_recv()
        for hx in range(2):
            for xl in range(2):
                both = acc[core, j, hx, xl] + crecv[j, hx, xl]
                acc[core, j, hx, xl] = both
                sx[j, hx, xl] = both[:, :, 0:8].reshape(4, 16, slab).astype(BF16)
                for yy in range(4):
                    sy[j, yy, hx, xl] = both[yy, :, 8:16].reshape(16, slab).astype(BF16)
        for k in (2, 1, 3):
            x1(j, k).start()
            y1(j, k).start()

    def second_sum(j):
        for k in (1, 2, 3):
            x1(j, k).wait_recv()
        mine = acc[core, j, x_hi, x_lo, :, :, 0:8].reshape(4, 16, slab)
        for k in range(3):
            mine = mine + rx[j, k].astype(F32)
        acc[core, j, x_hi, x_lo, :, :, 0:8] = mine.reshape(4, 2, 8, slab)
        s2y[j] = mine.astype(BF16)
        for k in (2, 1, 3):
            y2(j, k).start()
        for k in (1, 2, 3):
            y1(j, k).wait_recv()
        other = acc[core, j, :, :, y, :, 8:16].reshape(2, 2, 16, slab)
        for k in range(3):
            other = other + ry[j, k].astype(F32)
        acc[core, j, :, :, y, :, 8:16] = other.reshape(2, 2, 2, 8, slab)
        s2x[j] = other.astype(BF16)
        for k in (2, 1, 3):
            x2(j, k).start()

    def third_sum(j):
        for k in (1, 2, 3):
            y2(j, k).wait_recv()
            x2(j, k).wait_recv()
        upper = acc[core, j, x_hi, x_lo, y, :, 0:8].reshape(16, slab)
        lower = acc[core, j, x_hi, x_lo, y, :, 8:16].reshape(16, slab)
        for k in range(3):
            upper = upper + r2y[j, k].astype(F32)
            lower = lower + r2x[j, k].astype(F32)
        for sub in range(2):
            zs[j, sub, 0:8] = upper[sub * 8:sub * 8 + 8]
            zs[j, sub, 8:16] = lower[sub * 8:sub * 8 + 8]
        z3(j, 0).start()

        @pl.when(j % 4 < 3)
        def _():
            z3(j, 1).start()

    def pipeline(i, carry):
        @pl.when(i == 1)
        def _():
            st_merge(1, 2)

        @pl.when(i == 4)
        def _():
            first_sum(i - 1)
            st_merge(1, 3)
            direction_of(1)

        @pl.when(i < 8)
        def _():
            multiply(i)

        @pl.when((i >= 1) & (i < 9) & (i != 4))
        def _():
            first_sum(i - 1)

        @pl.when((i >= 4) & (i < 12))
        def _():
            second_sum(i - 4)

        @pl.when(i >= 6)
        def _():
            third_sum(i - 6)

        return carry

    lax.fori_loop(0, 14, pipeline, 0)
    grads = []
    for h in range(2):
        total = zs[h * 4 + 3, 1]
        for hop in range(7):
            z3(h * 4 + hop // 2, hop % 2).wait_recv()
            total = total + zr[h, hop]
        grads.append(total)
    grad = jnp.concatenate(grads, axis=0)

    scaled = grad * gslab[...]
    inner = jnp.sum(uslab[...] * scaled, axis=1, keepdims=True)
    iz[z] = jnp.broadcast_to(inner, (32, 128))
    for copy in to_voc(iz, iz_s, iz_r):
        copy.start()
    az[z] = attribute(scaled)
    for copy in to_voc(az, az_s, az_r):
        copy.start()
    add_voc(iz, iz_s, iz_r, ix, 1)
    add_voc(az, az_s, az_r, ax, 2)
    cross(bx, 0).wait_recv()
    cross(ix, 1).wait_recv()
    unit_dot = bx[0] + bx[1]
    mean = (ix[0] + ix[1]) * (1.0 / width)
    scale = 1.0 / rms_ref[...]
    cross(ax, 2).wait_recv()
    both = ax[0] + ax[1]
    for n in range(2):
        rows = slice(n * 16, n * 16 + 16)
        if n == 1:
            both = pltpu.roll(both, 64, 1)
            unit_dot = pltpu.roll(unit_dot, 64, 1)
        out_ref[rows] = ((both - unit_dot * mean[rows]) * scale[rows])[:, 0:64]

    for h in range(2):
        for k in (1, 2, 3):
            gy(h, k).wait_send()
        for kb in range(4):
            gx(h, kb).wait_send()
            gc(h, kb).wait_send()
            gd(h, kb).wait_send()
        for stage in range(4):
            for copy in st_copies(h, stage):
                copy.wait_send()

    def drain(j, carry):
        c_copy(j).wait_send()
        for k in (1, 2, 3):
            x1(j, k).wait_send()
            y1(j, k).wait_send()
            x2(j, k).wait_send()
            y2(j, k).wait_send()

        z3(j, 0).wait_send()

        @pl.when(j % 4 < 3)
        def _():
            z3(j, 1).wait_send()

        return carry

    lax.fori_loop(0, 8, drain, 0)
    for copy in to_voc(bz, bz_s, bz_r) + to_voc(az, az_s, az_r) + to_voc(iz, iz_s, iz_r):
        copy.wait_send()
    for n, over in enumerate((bx, ix, ax)):
        cross(over, n).wait_send()


def on_device(resid, norm_gain, unembed, targets, feat_ids, feat_acts, decoder):
    width = resid.shape[1]
    voc_cols = unembed.shape[1]
    slab, features = decoder.shape
    vm = pl.BlockSpec(memory_space=pltpu.VMEM)
    hbm = pl.BlockSpec(memory_space=pl.ANY)
    dma = pltpu.SemaphoreType.DMA
    projected = pl.pallas_call(
        body,
        out_shape=jax.ShapeDtypeStruct(feat_acts.shape, F32),
        in_specs=[vm, vm, hbm, vm, vm, hbm],
        out_specs=vm,
        scratch_shapes=[
            pltpu.VMEM(unembed.shape, BF16),
            pltpu.VMEM(decoder.shape, BF16),
            pltpu.VMEM((2, 2, 2, 4, 16, width), BF16),
            pltpu.VMEM((2, 256, voc_cols), F32),
            pltpu.VMEM((2, 256, voc_cols), BF16),
            pltpu.VMEM((32, 128), F32),
            pltpu.VMEM((1, width), F32),
            pltpu.VMEM((32, slab), F32),
            pltpu.VMEM((1, slab), F32),
            pltpu.VMEM((32, 128), jnp.int32),
            pltpu.VMEM((2, 5, 8, 128), F32),
            pltpu.VMEM((2, 14, 8, 128), F32),
            pltpu.VMEM((2, 8, 2, 2, 4, 2, 16, slab), F32),
            pltpu.VMEM((8, 2, 2, 4, 2, 16, slab), F32),
            pltpu.VMEM((8, 2, 2, 4, 16, slab), BF16),
            pltpu.VMEM((8, 4, 2, 2, 16, slab), BF16),
            pltpu.VMEM((8, 3, 4, 16, slab), BF16),
            pltpu.VMEM((8, 3, 2, 2, 16, slab), BF16),
            pltpu.VMEM((8, 2, 2, 16, slab), BF16),
            pltpu.VMEM((8, 4, 16, slab), BF16),
            pltpu.VMEM((8, 3, 16, slab), BF16),
            pltpu.VMEM((8, 3, 16, slab), BF16),
            pltpu.VMEM((8, 2, 16, slab), F32),
            pltpu.VMEM((2, 7, 16, slab), F32),
            pltpu.VMEM((8, 16, 128), F32),
            pltpu.VMEM((8, 16, 128), F32),
            pltpu.VMEM((8, 32, 128), F32),
            pltpu.VMEM((2, 16, 128), F32),
            pltpu.VMEM((2, 16, 128), F32),
            pltpu.VMEM((2, 32, 128), F32),
            dma((2,)),
            dma((2, 3)), dma((2, 3)),
            dma((2, 4)), dma((2, 4)),
            dma((2, 4)), dma((2, 4)),
            dma((2, 4)), dma((2, 4)),
            dma((2, 14)), dma((2, 14)),
            dma((8,)), dma((8,)),
            dma((8, 3)), dma((8, 3)),
            dma((8, 3)), dma((8, 3)),
            dma((8, 3)), dma((8, 3)),
            dma((8, 3)), dma((8, 3)),
            dma((2, 7)), dma((2, 7)),
            dma((7,)), dma((7,)),
            dma((7,)), dma((7,)),
            dma((7,)), dma((7,)),
            dma((3,)), dma((3,)),
        ],
        compiler_params=pltpu.CompilerParams(
            collective_id=0, has_side_effects=True, vmem_limit_bytes=60 * 1024 * 1024
        ),
    )(resid, norm_gain, unembed, targets.reshape(4, 128), feat_ids, decoder)
    return projected * feat_acts


def solution(mesh):
    placed = (
        P("tok", None),
        P(),
        P(None, ("tok", "voc")),
        P(),
        P("tok", None),
        P("tok", None),
        P("voc", None),
    )
    return jax.shard_map(
        on_device, mesh=mesh, in_specs=placed, out_specs=P("tok", None), check_vma=False
    )
```

```python
import functools

import jax
import jax.numpy as jnp
from jax import lax
from jax.experimental import pallas as pl
from jax.experimental.pallas import tpu as pltpu
from jax.sharding import PartitionSpec as P

EPSILON = 1e-06
MESH = pl.DeviceIdType.MESH
F32 = jnp.float32
BF16 = jnp.bfloat16
CHUNK = 2048
LAG2 = 4
LAG3 = 6


def body(
    resid_ref, gain_ref, unembed_hbm, targets_ref, ids_ref, decoder_hbm,
    out_ref,
    w_ref, dec_ref, nall, ebuf, dirbuf, rms_ref, gain_buf, uslab, gslab, idbuf,
    st_own, st_in, acc, crecv, sx, sy, rx, ry, s2x, s2y, r2x, r2y, zs, zr,
    bz, az, iz, bx, ax, ix,
    load_sem, gy_s, gy_r, gx_s, gx_r, gc_s, gc_r, gd_s, gd_r, st_s, st_r,
    c_s, c_r, x1_s, x1_r, y1_s, y1_r, x2_s, x2_r, y2_s, y2_r, z_s, z_r,
    bz_s, bz_r, az_s, az_r, iz_s, iz_r, fx_s, fx_r,
):
    tok = lax.axis_index("tok")
    voc = lax.axis_index("voc")
    x_lo = tok // 8
    y = (tok // 2) % 4
    core = tok % 2
    x_hi = voc // 8
    z = voc % 8
    x = x_hi * 2 + x_lo

    def device(xx, yy, zz, cc):
        return ((xx % 2) * 8 + yy * 2 + cc, (xx // 2) * 8 + zz)

    def x_peer(k):
        return device((x + k) % 4, y, z, core)

    def y_peer(k):
        return device(x, (y + k) % 4, z, core)

    def z_peer(k):
        return device(x, y, (z + k) % 8, core)

    sibling = device(x, y, z, 1 - core)

    def send(src, dst, s, r, peer):
        return pltpu.make_async_remote_copy(
            src_ref=src, dst_ref=dst, send_sem=s, recv_sem=r, device_id=peer, device_id_type=MESH
        )

    load_w = pltpu.make_async_copy(unembed_hbm, w_ref, load_sem.at[0])
    load_d = pltpu.make_async_copy(decoder_hbm, dec_ref, load_sem.at[1])
    load_w.start()
    load_d.start()
    barrier = pltpu.get_barrier_semaphore()
    peers = [sibling]
    peers += [x_peer(k) for k in (1, 2, 3)]
    peers += [y_peer(k) for k in (1, 2, 3)]
    peers += [z_peer(k) for k in range(1, 8)]
    plane = [(a, b) for a in range(4) for b in range(4) if a + b > 0]
    crossed = [device((x + a) % 4, (y + b) % 4, z, core) for a, b in plane]
    stat_peers = peers[0:1] + crossed + peers[7:14]
    peers = stat_peers
    for peer in peers:
        pl.semaphore_signal(barrier, inc=1, device_id=peer, device_id_type=MESH)

    hidden = resid_ref[...].astype(F32)
    width = hidden.shape[1]
    rms = jnp.sqrt(jnp.mean(hidden * hidden, axis=1, keepdims=True) + EPSILON)
    rms_ref[...] = jnp.broadcast_to(rms, rms_ref.shape)
    gain = gain_ref[...].reshape(1, width)
    gain_buf[...] = gain
    normed = (hidden / rms * gain).astype(BF16)
    for h in range(2):
        nall[h, x_lo, core, y] = normed[h * 16:h * 16 + 16]

    half = width // 2
    slab = half // 8
    pl.semaphore_wait(barrier, len(peers))

    def gy(h, k):
        part = nall.at[h, x_lo, core, y]
        return send(part, part, gy_s.at[h, k - 1], gy_r.at[h, k - 1], y_peer(k))

    def gx(h, kb, d):
        part = nall.at[h, x_lo, core, (y - kb + 4) % 4, :, pl.ds(d * half, half)]
        return send(part, part, gx_s.at[h, kb, d], gx_r.at[h, kb, d], x_peer(1 + 2 * d))

    def gc(h, kb):
        part = nall.at[h, x_lo, core, (y - kb + 4) % 4]
        return send(part, part, gc_s.at[h, kb], gc_r.at[h, kb], sibling)

    def gd(h, kb):
        part = nall.at[h, 1 - x_lo, core, (y - kb + 4) % 4]
        return send(part, part, gd_s.at[h, kb], gd_r.at[h, kb], sibling)

    def pass_on(h, k):
        gy(h, k).wait_recv()
        gx(h, k, 0).start()
        gx(h, k, 1).start()
        gc(h, k).start()

    def pass_over(h, kb):
        gx(h, kb, 0).wait_recv()
        gx(h, kb, 1).wait_recv()
        gd(h, kb).start()

    def gathered(h, own):
        for kb in (0, 1, 3, 2):
            (gc if own else gd)(h, kb).wait_recv()

    for k in (1, 3, 2):
        gy(0, k).start()
    for h in range(2):
        gx(h, 0, 0).start()
        gx(h, 0, 1).start()
    gc(0, 0).start()
    gc(1, 0).start()

    start = pl.multiple_of(x_hi * half, half)
    unit_half = resid_ref[:, pl.ds(start, half)].astype(F32) / rms
    gain_half = gain_buf[:, pl.ds(start, half)]
    for zz in range(8):
        @pl.when(z == zz)
        def _():
            uslab[...] = unit_half[:, zz * slab:(zz + 1) * slab]
            gslab[...] = gain_half[:, zz * slab:(zz + 1) * slab]
    st_own[...] = jnp.zeros_like(st_own)
    idbuf[...] = jnp.zeros_like(idbuf)
    idbuf[:, 0:64] = ids_ref[...]
    low_half = lax.broadcasted_iota(jnp.int32, (16, 128), 1) < 64

    def attribute(values):
        high = values.astype(BF16)
        low = (values - high.astype(F32)).astype(BF16)
        stacked = jnp.concatenate([high, low], axis=0)
        lanes = jnp.bitwise_and(idbuf[...], 127)
        tiles = jnp.right_shift(idbuf[...], 7)

        def step(n, picked):
            cols = pl.ds(pl.multiple_of(n * CHUNK, CHUNK), CHUNK)
            both = jnp.dot(stacked, dec_ref[:, cols], preferred_element_type=F32)
            dots = both[0:32] + both[32:64]
            for q in range(CHUNK // 128):
                got = jnp.take_along_axis(
                    dots[:, q * 128:(q + 1) * 128], lanes, axis=1, mode="promise_in_bounds"
                )
                picked = jnp.where(tiles == n * (CHUNK // 128) + q, got, picked)
            return picked

        picked = lax.fori_loop(0, dec_ref.shape[1] // CHUNK, step, jnp.zeros((32, 128), F32))
        return jnp.where(low_half, picked[0:16], pltpu.roll(picked[16:32], 64, 1))

    def to_voc(buf, s, r):
        return [send(buf.at[z], buf.at[z], s.at[k - 1], r.at[k - 1], z_peer(k)) for k in range(1, 8)]

    load_d.wait()
    bz[z] = attribute(uslab[...])
    for copy in to_voc(bz, bz_s, bz_r):
        copy.start()

    eye = lax.broadcasted_iota(jnp.int32, (128, 128), 0) == lax.broadcasted_iota(jnp.int32, (128, 128), 1)

    def to_row(col):
        return jnp.sum(jnp.where(eye, col, 0.0), axis=0, keepdims=True)

    def to_col(row):
        return jnp.sum(jnp.where(eye, row, 0.0), axis=1, keepdims=True)

    def logits_of(h, xl):
        rows = pl.ds(pl.multiple_of(xl * 128, 128), 128)
        left = nall[h, xl].reshape(128, width)

        def step(n, carry):
            cols = pl.ds(pl.multiple_of(n * 256, 256), 256)
            ebuf[h, rows, cols] = jnp.dot(left, w_ref[:, cols], preferred_element_type=F32)
            return carry

        lax.fori_loop(0, ebuf.shape[2] // 256, step, 0)
        part = ebuf[h, rows]
        top = jnp.max(part, axis=1, keepdims=True)
        part = jnp.exp(part - top)
        ebuf[h, rows] = part
        st_own[h, 0, pl.ds(xl, 1)] = to_row(top)
        st_own[h, 0, pl.ds(2 + xl, 1)] = to_row(jnp.sum(part, axis=1, keepdims=True))

    firsts = [0, 1, 16, 23]

    def st_copies(h, stage):
        return [
            send(st_own.at[h, stage], st_in.at[h, n], st_s.at[h, n], st_r.at[h, n], stat_peers[n])
            for n in range(firsts[stage], firsts[stage + 1])
        ]

    def st_send(h, stage):
        for copy in st_copies(h, stage):
            copy.start()

    def st_merge(h, stage):
        for copy in st_copies(h, stage):
            copy.wait_recv()
        tiles = [st_own[h, stage]] + [st_in[h, n] for n in range(firsts[stage], firsts[stage + 1])]
        merged = functools.reduce(jnp.maximum, [t[0:2] for t in tiles])
        st_own[h, stage + 1, 0:2] = merged
        st_own[h, stage + 1, 2:4] = sum(t[2:4] * jnp.exp(t[0:2] - merged) for t in tiles)
        if stage < 2:
            st_send(h, stage + 1)

    voc_cols = w_ref.shape[1]

    def direction_of(h):
        scale = jnp.exp(st_own[h, 0, 0:2] - st_own[h, 3, 0:2]) / st_own[h, 3, 2:4]
        lane = lax.broadcasted_iota(jnp.int32, (128, voc_cols), 1).astype(F32)
        rel = (targets_ref[...] - (tok * 16 + voc) * voc_cols).astype(F32)
        cols = [to_col(rel[n:n + 1]) for n in range(4)]
        for q in range(2):
            prob = ebuf[h, pl.ds(q * 128, 128)] * to_col(scale[q:q + 1])
            parts = []
            for cc in range(2):
                for yy in range(4):
                    first = (yy % 2) * 64 + cc * 32 + h * 16
                    parts.append(cols[q * 2 + yy // 2][first:first + 16])
            hot = jnp.where(lane == jnp.concatenate(parts, axis=0), 1.0, 0.0)
            dirbuf[h, pl.ds(q * 128, 128)] = (hot - prob).astype(BF16)

    for k in (1, 3, 2):
        gy(1, k).start()
    pass_on(0, 1)
    pass_on(0, 3)
    pass_over(0, 0)
    pass_on(0, 2)
    pass_over(1, 0)
    pass_over(0, 1)
    pass_over(0, 3)
    pass_on(1, 1)
    pass_on(1, 3)
    pass_over(0, 2)
    pass_on(1, 2)
    load_w.wait()
    gathered(0, True)
    logits_of(0, x_lo)
    gathered(0, False)
    logits_of(0, 1 - x_lo)
    st_send(0, 0)
    pass_over(1, 1)
    pass_over(1, 3)
    st_merge(0, 0)
    pass_over(1, 2)
    gathered(1, True)
    logits_of(1, x_lo)
    gathered(1, False)
    logits_of(1, 1 - x_lo)
    st_send(1, 0)
    st_merge(1, 0)
    st_merge(0, 1)

    def cross(buf, n):
        return send(buf.at[0], buf.at[1], fx_s.at[n], fx_r.at[n], x_peer(2))

    def add_voc(buf, s, r, over, n):
        for copy in to_voc(buf, s, r):
            copy.wait_recv()
        over[0] = sum(buf[m] for m in range(8))
        cross(over, n).start()

    add_voc(bz, bz_s, bz_r, bx, 0)
    st_merge(0, 2)
    direction_of(0)

    def c_copy(j):
        return send(acc.at[1 - core, j], crecv.at[j], c_s.at[j], c_r.at[j], sibling)

    def x1(j, k):
        to = (x + k) % 4
        return send(sx.at[j, to // 2, to % 2], rx.at[j, k - 1], x1_s.at[j, k - 1], x1_r.at[j, k - 1], x_peer(k))

    def y1(j, k):
        return send(sy.at[j, (y + k) % 4], ry.at[j, k - 1], y1_s.at[j, k - 1], y1_r.at[j, k - 1], y_peer(k))

    def x2(j, k):
        to = (x + k) % 4
        return send(s2x.at[j, to // 2, to % 2], r2x.at[j, k - 1], x2_s.at[j, k - 1], x2_r.at[j, k - 1], x_peer(k))

    def y2(j, k):
        return send(s2y.at[j, (y + k) % 4], r2y.at[j, k - 1], y2_s.at[j, k - 1], y2_r.at[j, k - 1], y_peer(k))

    def z3(j, sub):
        hop = 2 * (j % 4) + sub
        slot = (j // 4, hop)
        return send(zs.at[j, sub], zr.at[slot], z_s.at[slot], z_r.at[slot], z_peer(hop + 1))

    def multiply(j):
        for sub in range(2):
            group = (z + 1 + 2 * (j % 4) + sub) % 8
            for hx in range(2):
                rows = pl.ds(pl.multiple_of(hx * half + group * slab, 32), slab)
                part = lax.dot_general(
                    dirbuf[j // 4], w_ref[rows, :], (((1,), (1,)), ((), ())), preferred_element_type=F32
                )
                for q in range(4):
                    acc[q % 2, j, hx, q // 2, :, sub] = part[q * 64:(q + 1) * 64].reshape(4, 16, slab)
        c_copy(j).start()

    def first_sum(j):
        c_copy(j).wait_recv()
        for hx in range(2):
            for xl in range(2):
                both = acc[core, j, hx, xl] + crecv[j, hx, xl]
                acc[core, j, hx, xl] = both
                sx[j, hx, xl] = both[:, :, 0:8].reshape(4, 16, slab).astype(BF16)
                for yy in range(4):
                    sy[j, yy, hx, xl] = both[yy, :, 8:16].reshape(16, slab).astype(BF16)
        for k in (2, 1, 3):
            x1(j, k).start()
            y1(j, k).start()

    def second_sum(j):
        for k in (1, 2, 3):
            x1(j, k).wait_recv()
        mine = acc[core, j, x_hi, x_lo, :, :, 0:8].reshape(4, 16, slab)
        for k in range(3):
            mine = mine + rx[j, k].astype(F32)
        acc[core, j, x_hi, x_lo, :, :, 0:8] = mine.reshape(4, 2, 8, slab)
        s2y[j] = mine.astype(BF16)
        for k in (2, 1, 3):
            y2(j, k).start()
        for k in (1, 2, 3):
            y1(j, k).wait_recv()
        other = acc[core, j, :, :, y, :, 8:16].reshape(2, 2, 16, slab)
        for k in range(3):
            other = other + ry[j, k].astype(F32)
        acc[core, j, :, :, y, :, 8:16] = other.reshape(2, 2, 2, 8, slab)
        s2x[j] = other.astype(BF16)
        for k in (2, 1, 3):
            x2(j, k).start()

    def third_sum(j):
        for k in (1, 2, 3):
            y2(j, k).wait_recv()
            x2(j, k).wait_recv()
        upper = acc[core, j, x_hi, x_lo, y, :, 0:8].reshape(16, slab)
        lower = acc[core, j, x_hi, x_lo, y, :, 8:16].reshape(16, slab)
        for k in range(3):
            upper = upper + r2y[j, k].astype(F32)
            lower = lower + r2x[j, k].astype(F32)
        for sub in range(2):
            zs[j, sub, 0:8] = upper[sub * 8:sub * 8 + 8]
            zs[j, sub, 8:16] = lower[sub * 8:sub * 8 + 8]
        z3(j, 0).start()

        @pl.when(j % 4 < 3)
        def _():
            z3(j, 1).start()

    def pipeline(i, carry):
        @pl.when(i == 1)
        def _():
            st_merge(1, 1)

        @pl.when(i == 4)
        def _():
            first_sum(i - 1)
            st_merge(1, 2)
            direction_of(1)

        @pl.when(i < 8)
        def _():
            multiply(i)

        @pl.when((i >= 1) & (i < 9) & (i != 4))
        def _():
            first_sum(i - 1)

        @pl.when((i >= LAG2) & (i < 8 + LAG2))
        def _():
            second_sum(i - LAG2)

        @pl.when(i >= LAG3)
        def _():
            third_sum(i - LAG3)

        return carry

    lax.fori_loop(0, 8 + LAG3, pipeline, 0)
    grads = []
    for h in range(2):
        total = zs[h * 4 + 3, 1]
        for hop in range(7):
            z3(h * 4 + hop // 2, hop % 2).wait_recv()
            total = total + zr[h, hop]
        grads.append(total)
    grad = jnp.concatenate(grads, axis=0)

    scaled = grad * gslab[...]
    inner = jnp.sum(uslab[...] * scaled, axis=1, keepdims=True)
    iz[z] = jnp.broadcast_to(inner, (32, 128))
    for copy in to_voc(iz, iz_s, iz_r):
        copy.start()
    az[z] = attribute(scaled)
    for copy in to_voc(az, az_s, az_r):
        copy.start()
    add_voc(iz, iz_s, iz_r, ix, 1)
    for h in range(2):
        for k in (1, 2, 3):
            gy(h, k).wait_send()
        for kb in range(4):
            gx(h, kb, 0).wait_send()
            gx(h, kb, 1).wait_send()
            gc(h, kb).wait_send()
            gd(h, kb).wait_send()
        for stage in range(3):
            for copy in st_copies(h, stage):
                copy.wait_send()

    def drain(j, carry):
        c_copy(j).wait_send()
        for k in (1, 2, 3):
            x1(j, k).wait_send()
            y1(j, k).wait_send()
            x2(j, k).wait_send()
            y2(j, k).wait_send()

        z3(j, 0).wait_send()

        @pl.when(j % 4 < 3)
        def _():
            z3(j, 1).wait_send()

        return carry

    lax.fori_loop(0, 8, drain, 0)
    add_voc(az, az_s, az_r, ax, 2)
    cross(bx, 0).wait_recv()
    cross(ix, 1).wait_recv()
    unit_dot = bx[0] + bx[1]
    mean = (ix[0] + ix[1]) * (1.0 / width)
    scale = 1.0 / rms_ref[...]
    cross(ax, 2).wait_recv()
    both = ax[0] + ax[1]
    for n in range(2):
        rows = slice(n * 16, n * 16 + 16)
        if n == 1:
            both = pltpu.roll(both, 64, 1)
            unit_dot = pltpu.roll(unit_dot, 64, 1)
        out_ref[rows] = ((both - unit_dot * mean[rows]) * scale[rows])[:, 0:64]

    for copy in to_voc(bz, bz_s, bz_r) + to_voc(az, az_s, az_r) + to_voc(iz, iz_s, iz_r):
        copy.wait_send()
    for n, over in enumerate((bx, ix, ax)):
        cross(over, n).wait_send()


def on_device(resid, norm_gain, unembed, targets, feat_ids, feat_acts, decoder):
    width = resid.shape[1]
    voc_cols = unembed.shape[1]
    slab, features = decoder.shape
    vm = pl.BlockSpec(memory_space=pltpu.VMEM)
    hbm = pl.BlockSpec(memory_space=pl.ANY)
    dma = pltpu.SemaphoreType.DMA
    projected = pl.pallas_call(
        body,
        out_shape=jax.ShapeDtypeStruct(feat_acts.shape, F32),
        in_specs=[vm, vm, hbm, vm, vm, hbm],
        out_specs=vm,
        scratch_shapes=[
            pltpu.VMEM(unembed.shape, BF16),
            pltpu.VMEM(decoder.shape, BF16),
            pltpu.VMEM((2, 2, 2, 4, 16, width), BF16),
            pltpu.VMEM((2, 256, voc_cols), F32),
            pltpu.VMEM((2, 256, voc_cols), BF16),
            pltpu.VMEM((32, 128), F32),
            pltpu.VMEM((1, width), F32),
            pltpu.VMEM((32, slab), F32),
            pltpu.VMEM((1, slab), F32),
            pltpu.VMEM((32, 128), jnp.int32),
            pltpu.VMEM((2, 4, 8, 128), F32),
            pltpu.VMEM((2, 23, 8, 128), F32),
            pltpu.VMEM((2, 8, 2, 2, 4, 2, 16, slab), F32),
            pltpu.VMEM((8, 2, 2, 4, 2, 16, slab), F32),
            pltpu.VMEM((8, 2, 2, 4, 16, slab), BF16),
            pltpu.VMEM((8, 4, 2, 2, 16, slab), BF16),
            pltpu.VMEM((8, 3, 4, 16, slab), BF16),
            pltpu.VMEM((8, 3, 2, 2, 16, slab), BF16),
            pltpu.VMEM((8, 2, 2, 16, slab), BF16),
            pltpu.VMEM((8, 4, 16, slab), BF16),
            pltpu.VMEM((8, 3, 16, slab), BF16),
            pltpu.VMEM((8, 3, 16, slab), BF16),
            pltpu.VMEM((8, 2, 16, slab), F32),
            pltpu.VMEM((2, 7, 16, slab), F32),
            pltpu.VMEM((8, 16, 128), F32),
            pltpu.VMEM((8, 16, 128), F32),
            pltpu.VMEM((8, 32, 128), F32),
            pltpu.VMEM((2, 16, 128), F32),
            pltpu.VMEM((2, 16, 128), F32),
            pltpu.VMEM((2, 32, 128), F32),
            dma((2,)),
            dma((2, 3)), dma((2, 3)),
            dma((2, 4, 2)), dma((2, 4, 2)),
            dma((2, 4)), dma((2, 4)),
            dma((2, 4)), dma((2, 4)),
            dma((2, 23)), dma((2, 23)),
            dma((8,)), dma((8,)),
            dma((8, 3)), dma((8, 3)),
            dma((8, 3)), dma((8, 3)),
            dma((8, 3)), dma((8, 3)),
            dma((8, 3)), dma((8, 3)),
            dma((2, 7)), dma((2, 7)),
            dma((7,)), dma((7,)),
            dma((7,)), dma((7,)),
            dma((7,)), dma((7,)),
            dma((3,)), dma((3,)),
        ],
        compiler_params=pltpu.CompilerParams(
            collective_id=0, has_side_effects=True, vmem_limit_bytes=60 * 1024 * 1024
        ),
    )(resid, norm_gain, unembed, targets.reshape(4, 128), feat_ids, decoder)
    return projected * feat_acts


def solution(mesh):
    placed = (
        P("tok", None),
        P(),
        P(None, ("tok", "voc")),
        P(),
        P("tok", None),
        P("tok", None),
        P("voc", None),
    )
    return jax.shard_map(
        on_device, mesh=mesh, in_specs=placed, out_specs=P("tok", None), check_vma=False
    )
```

```python
import functools

import jax
import jax.numpy as jnp
from jax import lax
from jax.experimental import pallas as pl
from jax.experimental.pallas import tpu as pltpu
from jax.sharding import PartitionSpec as P

EPSILON = 1e-06
MESH = pl.DeviceIdType.MESH
F32 = jnp.float32
BF16 = jnp.bfloat16
CHUNK = 8192
LAG2 = 4
LAG3 = 6


def body(
    resid_ref, gain_ref, unembed_hbm, targets_ref, ids_ref, decoder_hbm,
    out_ref,
    w_ref, dec_ref, nall, ebuf, dirbuf, rms_ref, gain_buf, uslab, gslab, idbuf,
    st_own, st_in, acc, crecv, sx, sy, rx, ry, s2x, s2y, r2x, r2y, zs, zr,
    bz, az, iz, bx, ax, ix,
    load_sem, gy_s, gy_r, gx_s, gx_r, gc_s, gc_r, gd_s, gd_r, st_s, st_r,
    c_s, c_r, x1_s, x1_r, y1_s, y1_r, x2_s, x2_r, y2_s, y2_r, z_s, z_r,
    bz_s, bz_r, az_s, az_r, iz_s, iz_r, fx_s, fx_r,
):
    tok = lax.axis_index("tok")
    voc = lax.axis_index("voc")
    x_lo = tok // 8
    y = (tok // 2) % 4
    core = tok % 2
    x_hi = voc // 8
    z = voc % 8
    x = x_hi * 2 + x_lo

    def device(xx, yy, zz, cc):
        return ((xx % 2) * 8 + yy * 2 + cc, (xx // 2) * 8 + zz)

    def x_peer(k):
        return device((x + k) % 4, y, z, core)

    def y_peer(k):
        return device(x, (y + k) % 4, z, core)

    def z_peer(k):
        return device(x, y, (z + k) % 8, core)

    sibling = device(x, y, z, 1 - core)

    def send(src, dst, s, r, peer):
        return pltpu.make_async_remote_copy(
            src_ref=src, dst_ref=dst, send_sem=s, recv_sem=r, device_id=peer, device_id_type=MESH
        )

    load_w = pltpu.make_async_copy(unembed_hbm, w_ref, load_sem.at[0])
    load_d = pltpu.make_async_copy(decoder_hbm, dec_ref, load_sem.at[1])
    load_w.start()
    load_d.start()
    barrier = pltpu.get_barrier_semaphore()
    peers = [sibling]
    peers += [x_peer(k) for k in (1, 2, 3)]
    peers += [y_peer(k) for k in (1, 2, 3)]
    peers += [z_peer(k) for k in range(1, 8)]
    plane = [(a, b) for a in range(4) for b in range(4) if a + b > 0]
    crossed = [device((x + a) % 4, (y + b) % 4, z, core) for a, b in plane]
    stat_peers = peers[0:1] + crossed + peers[7:14]
    peers = stat_peers
    for peer in peers:
        pl.semaphore_signal(barrier, inc=1, device_id=peer, device_id_type=MESH)

    hidden = resid_ref[...].astype(F32)
    width = hidden.shape[1]
    rms = jnp.sqrt(jnp.mean(hidden * hidden, axis=1, keepdims=True) + EPSILON)
    rms_ref[...] = jnp.broadcast_to(rms, rms_ref.shape)
    gain = gain_ref[...].reshape(1, width)
    gain_buf[...] = gain
    normed = (hidden / rms * gain).astype(BF16)
    for h in range(2):
        nall[h, x_lo, core, y] = normed[h * 16:h * 16 + 16]

    half = width // 2
    slab = half // 8
    pl.semaphore_wait(barrier, len(peers))

    def gy(h, k):
        part = nall.at[h, x_lo, core, y]
        return send(part, part, gy_s.at[h, k - 1], gy_r.at[h, k - 1], y_peer(k))

    def gx(h, kb, d):
        part = nall.at[h, x_lo, core, (y - kb + 4) % 4, :, pl.ds(d * half, half)]
        return send(part, part, gx_s.at[h, kb, d], gx_r.at[h, kb, d], x_peer(1 + 2 * d))

    def gc(h, kb):
        part = nall.at[h, x_lo, core, (y - kb + 4) % 4]
        return send(part, part, gc_s.at[h, kb], gc_r.at[h, kb], sibling)

    def gd(h, kb):
        part = nall.at[h, 1 - x_lo, core, (y - kb + 4) % 4]
        return send(part, part, gd_s.at[h, kb], gd_r.at[h, kb], sibling)

    def pass_on(h, k):
        gy(h, k).wait_recv()
        gx(h, k, 0).start()
        gx(h, k, 1).start()
        gc(h, k).start()

    def pass_over(h, kb):
        gx(h, kb, 0).wait_recv()
        gx(h, kb, 1).wait_recv()
        gd(h, kb).start()

    def gathered(h, own):
        for kb in (0, 1, 3, 2):
            (gc if own else gd)(h, kb).wait_recv()

    for k in (1, 3, 2):
        gy(0, k).start()
    for h in range(2):
        gx(h, 0, 0).start()
        gx(h, 0, 1).start()
    gc(0, 0).start()
    gc(1, 0).start()

    start = pl.multiple_of(x_hi * half, half)
    unit_half = resid_ref[:, pl.ds(start, half)].astype(F32) / rms
    gain_half = gain_buf[:, pl.ds(start, half)]
    for zz in range(8):
        @pl.when(z == zz)
        def _():
            uslab[...] = unit_half[:, zz * slab:(zz + 1) * slab]
            gslab[...] = gain_half[:, zz * slab:(zz + 1) * slab]
    st_own[...] = jnp.zeros_like(st_own)
    idbuf[...] = jnp.zeros_like(idbuf)
    idbuf[:, 0:64] = ids_ref[...]
    low_half = lax.broadcasted_iota(jnp.int32, (16, 128), 1) < 64

    def attribute(values):
        high = values.astype(BF16)
        low = (values - high.astype(F32)).astype(BF16)
        stacked = jnp.concatenate([high, low], axis=0)
        lanes = jnp.bitwise_and(idbuf[...], 127)
        tiles = jnp.right_shift(idbuf[...], 7)

        def step(n, picked):
            cols = pl.ds(pl.multiple_of(n * CHUNK, CHUNK), CHUNK)
            both = jnp.dot(stacked, dec_ref[:, cols], preferred_element_type=F32)
            dots = both[0:32] + both[32:64]
            for q in range(CHUNK // 128):
                got = jnp.take_along_axis(
                    dots[:, q * 128:(q + 1) * 128], lanes, axis=1, mode="promise_in_bounds"
                )
                picked = jnp.where(tiles == n * (CHUNK // 128) + q, got, picked)
            return picked

        picked = lax.fori_loop(0, dec_ref.shape[1] // CHUNK, step, jnp.zeros((32, 128), F32))
        return jnp.where(low_half, picked[0:16], pltpu.roll(picked[16:32], 64, 1))

    def to_voc(buf, s, r):
        return [send(buf.at[z], buf.at[z], s.at[k - 1], r.at[k - 1], z_peer(k)) for k in range(1, 8)]

    load_d.wait()
    bz[z] = attribute(uslab[...])
    for copy in to_voc(bz, bz_s, bz_r):
        copy.start()

    eye = lax.broadcasted_iota(jnp.int32, (128, 128), 0) == lax.broadcasted_iota(jnp.int32, (128, 128), 1)

    def to_row(col):
        return jnp.sum(jnp.where(eye, col, 0.0), axis=0, keepdims=True)

    def to_col(row):
        return jnp.sum(jnp.where(eye, row, 0.0), axis=1, keepdims=True)

    def logits_of(h, xl):
        rows = pl.ds(pl.multiple_of(xl * 128, 128), 128)
        left = nall[h, xl].reshape(128, width)

        def step(n, carry):
            cols = pl.ds(pl.multiple_of(n * 256, 256), 256)
            ebuf[h, rows, cols] = jnp.dot(left, w_ref[:, cols], preferred_element_type=F32)
            return carry

        lax.fori_loop(0, ebuf.shape[2] // 256, step, 0)
        part = ebuf[h, rows]
        top = jnp.max(part, axis=1, keepdims=True)
        part = jnp.exp(part - top)
        ebuf[h, rows] = part
        st_own[h, 0, pl.ds(xl, 1)] = to_row(top)
        st_own[h, 0, pl.ds(2 + xl, 1)] = to_row(jnp.sum(part, axis=1, keepdims=True))

    firsts = [0, 1, 16, 23]

    def st_copies(h, stage):
        return [
            send(st_own.at[h, stage], st_in.at[h, n], st_s.at[h, n], st_r.at[h, n], stat_peers[n])
            for n in range(firsts[stage], firsts[stage + 1])
        ]

    def st_send(h, stage):
        for copy in st_copies(h, stage):
            copy.start()

    def st_merge(h, stage):
        for copy in st_copies(h, stage):
            copy.wait_recv()
        tiles = [st_own[h, stage]] + [st_in[h, n] for n in range(firsts[stage], firsts[stage + 1])]
        merged = functools.reduce(jnp.maximum, [t[0:2] for t in tiles])
        st_own[h, stage + 1, 0:2] = merged
        st_own[h, stage + 1, 2:4] = sum(t[2:4] * jnp.exp(t[0:2] - merged) for t in tiles)
        if stage < 2:
            st_send(h, stage + 1)

    voc_cols = w_ref.shape[1]

    def direction_of(h):
        scale = jnp.exp(st_own[h, 0, 0:2] - st_own[h, 3, 0:2]) / st_own[h, 3, 2:4]
        lane = lax.broadcasted_iota(jnp.int32, (128, voc_cols), 1).astype(F32)
        rel = (targets_ref[...] - (tok * 16 + voc) * voc_cols).astype(F32)
        cols = [to_col(rel[n:n + 1]) for n in range(4)]
        for q in range(2):
            prob = ebuf[h, pl.ds(q * 128, 128)] * to_col(scale[q:q + 1])
            parts = []
            for cc in range(2):
                for yy in range(4):
                    first = (yy % 2) * 64 + cc * 32 + h * 16
                    parts.append(cols[q * 2 + yy // 2][first:first + 16])
            hot = jnp.where(lane == jnp.concatenate(parts, axis=0), 1.0, 0.0)
            dirbuf[h, pl.ds(q * 128, 128)] = (hot - prob).astype(BF16)

    for k in (1, 3, 2):
        gy(1, k).start()
    pass_on(0, 1)
    pass_on(0, 3)
    pass_over(0, 0)
    pass_on(0, 2)
    pass_over(1, 0)
    pass_over(0, 1)
    pass_over(0, 3)
    pass_on(1, 1)
    pass_on(1, 3)
    pass_over(0, 2)
    pass_on(1, 2)
    load_w.wait()
    gathered(0, True)
    logits_of(0, x_lo)
    gathered(0, False)
    logits_of(0, 1 - x_lo)
    st_send(0, 0)
    pass_over(1, 1)
    pass_over(1, 3)
    st_merge(0, 0)
    pass_over(1, 2)
    gathered(1, True)
    logits_of(1, x_lo)
    gathered(1, False)
    logits_of(1, 1 - x_lo)
    st_send(1, 0)
    st_merge(1, 0)
    st_merge(0, 1)

    def cross(buf, n):
        return send(buf.at[0], buf.at[1], fx_s.at[n], fx_r.at[n], x_peer(2))

    def add_voc(buf, s, r, over, n):
        for copy in to_voc(buf, s, r):
            copy.wait_recv()
        over[0] = sum(buf[m] for m in range(8))
        cross(over, n).start()

    add_voc(bz, bz_s, bz_r, bx, 0)
    st_merge(0, 2)
    direction_of(0)

    def c_copy(j):
        return send(acc.at[1 - core, j], crecv.at[j], c_s.at[j], c_r.at[j], sibling)

    def x1(j, k):
        to = (x + k) % 4
        return send(sx.at[j, to // 2, to % 2], rx.at[j, k - 1], x1_s.at[j, k - 1], x1_r.at[j, k - 1], x_peer(k))

    def y1(j, k):
        return send(sy.at[j, (y + k) % 4], ry.at[j, k - 1], y1_s.at[j, k - 1], y1_r.at[j, k - 1], y_peer(k))

    def x2(j, k):
        to = (x + k) % 4
        return send(s2x.at[j, to // 2, to % 2], r2x.at[j, k - 1], x2_s.at[j, k - 1], x2_r.at[j, k - 1], x_peer(k))

    def y2(j, k):
        return send(s2y.at[j, (y + k) % 4], r2y.at[j, k - 1], y2_s.at[j, k - 1], y2_r.at[j, k - 1], y_peer(k))

    def z3(j, sub):
        hop = 2 * (j % 4) + sub
        slot = (j // 4, hop)
        return send(zs.at[j, sub], zr.at[slot], z_s.at[slot], z_r.at[slot], z_peer(hop + 1))

    def multiply(j):
        for sub in range(2):
            group = (z + 1 + 2 * (j % 4) + sub) % 8
            for hx in range(2):
                rows = pl.ds(pl.multiple_of(hx * half + group * slab, 32), slab)
                part = lax.dot_general(
                    dirbuf[j // 4], w_ref[rows, :], (((1,), (1,)), ((), ())), preferred_element_type=F32
                )
                for q in range(4):
                    acc[q % 2, j, hx, q // 2, :, sub] = part[q * 64:(q + 1) * 64].reshape(4, 16, slab)
        c_copy(j).start()

    def first_sum(j):
        c_copy(j).wait_recv()
        for hx in range(2):
            for xl in range(2):
                both = acc[core, j, hx, xl] + crecv[j, hx, xl]
                acc[core, j, hx, xl] = both
                sx[j, hx, xl] = both[:, :, 0:8].reshape(4, 16, slab).astype(BF16)
                for yy in range(4):
                    sy[j, yy, hx, xl] = both[yy, :, 8:16].reshape(16, slab).astype(BF16)
        for k in (2, 1, 3):
            x1(j, k).start()
            y1(j, k).start()

    def second_sum(j):
        for k in (1, 2, 3):
            x1(j, k).wait_recv()
        mine = acc[core, j, x_hi, x_lo, :, :, 0:8].reshape(4, 16, slab)
        for k in range(3):
            mine = mine + rx[j, k].astype(F32)
        acc[core, j, x_hi, x_lo, :, :, 0:8] = mine.reshape(4, 2, 8, slab)
        s2y[j] = mine.astype(BF16)
        for k in (2, 1, 3):
            y2(j, k).start()
        for k in (1, 2, 3):
            y1(j, k).wait_recv()
        other = acc[core, j, :, :, y, :, 8:16].reshape(2, 2, 16, slab)
        for k in range(3):
            other = other + ry[j, k].astype(F32)
        acc[core, j, :, :, y, :, 8:16] = other.reshape(2, 2, 2, 8, slab)
        s2x[j] = other.astype(BF16)
        for k in (2, 1, 3):
            x2(j, k).start()

    def third_sum(j):
        for k in (1, 2, 3):
            y2(j, k).wait_recv()
            x2(j, k).wait_recv()
        upper = acc[core, j, x_hi, x_lo, y, :, 0:8].reshape(16, slab)
        lower = acc[core, j, x_hi, x_lo, y, :, 8:16].reshape(16, slab)
        for k in range(3):
            upper = upper + r2y[j, k].astype(F32)
            lower = lower + r2x[j, k].astype(F32)
        for sub in range(2):
            zs[j, sub, 0:8] = upper[sub * 8:sub * 8 + 8]
            zs[j, sub, 8:16] = lower[sub * 8:sub * 8 + 8]
        z3(j, 0).start()

        @pl.when(j % 4 < 3)
        def _():
            z3(j, 1).start()

    def pipeline(i, carry):
        @pl.when(i == 1)
        def _():
            st_merge(1, 1)

        @pl.when(i == 4)
        def _():
            first_sum(i - 1)
            st_merge(1, 2)
            direction_of(1)

        @pl.when(i < 8)
        def _():
            multiply(i)

        @pl.when((i >= 1) & (i < 9) & (i != 4))
        def _():
            first_sum(i - 1)

        @pl.when((i >= LAG2) & (i < 8 + LAG2))
        def _():
            second_sum(i - LAG2)

        @pl.when(i >= LAG3)
        def _():
            third_sum(i - LAG3)

        return carry

    lax.fori_loop(0, 8 + LAG3, pipeline, 0)
    grads = []
    for h in range(2):
        total = zs[h * 4 + 3, 1]
        for hop in range(7):
            z3(h * 4 + hop // 2, hop % 2).wait_recv()
            total = total + zr[h, hop]
        grads.append(total)
    grad = jnp.concatenate(grads, axis=0)

    scaled = grad * gslab[...]
    inner = jnp.sum(uslab[...] * scaled, axis=1, keepdims=True)
    iz[z] = jnp.broadcast_to(inner, (32, 128))
    for copy in to_voc(iz, iz_s, iz_r):
        copy.start()
    az[z] = attribute(scaled)
    for copy in to_voc(az, az_s, az_r):
        copy.start()
    add_voc(iz, iz_s, iz_r, ix, 1)
    for h in range(2):
        for k in (1, 2, 3):
            gy(h, k).wait_send()
        for kb in range(4):
            gx(h, kb, 0).wait_send()
            gx(h, kb, 1).wait_send()
            gc(h, kb).wait_send()
            gd(h, kb).wait_send()
        for stage in range(3):
            for copy in st_copies(h, stage):
                copy.wait_send()

    def drain(j, carry):
        c_copy(j).wait_send()
        for k in (1, 2, 3):
            x1(j, k).wait_send()
            y1(j, k).wait_send()
            x2(j, k).wait_send()
            y2(j, k).wait_send()

        z3(j, 0).wait_send()

        @pl.when(j % 4 < 3)
        def _():
            z3(j, 1).wait_send()

        return carry

    lax.fori_loop(0, 8, drain, 0)
    add_voc(az, az_s, az_r, ax, 2)
    cross(bx, 0).wait_recv()
    cross(ix, 1).wait_recv()
    unit_dot = bx[0] + bx[1]
    mean = (ix[0] + ix[1]) * (1.0 / width)
    scale = 1.0 / rms_ref[...]
    cross(ax, 2).wait_recv()
    both = ax[0] + ax[1]
    for n in range(2):
        rows = slice(n * 16, n * 16 + 16)
        if n == 1:
            both = pltpu.roll(both, 64, 1)
            unit_dot = pltpu.roll(unit_dot, 64, 1)
        out_ref[rows] = ((both - unit_dot * mean[rows]) * scale[rows])[:, 0:64]

    for copy in to_voc(bz, bz_s, bz_r) + to_voc(az, az_s, az_r) + to_voc(iz, iz_s, iz_r):
        copy.wait_send()
    for n, over in enumerate((bx, ix, ax)):
        cross(over, n).wait_send()


def on_device(resid, norm_gain, unembed, targets, feat_ids, feat_acts, decoder):
    width = resid.shape[1]
    voc_cols = unembed.shape[1]
    slab, features = decoder.shape
    vm = pl.BlockSpec(memory_space=pltpu.VMEM)
    hbm = pl.BlockSpec(memory_space=pl.ANY)
    dma = pltpu.SemaphoreType.DMA
    projected = pl.pallas_call(
        body,
        out_shape=jax.ShapeDtypeStruct(feat_acts.shape, F32),
        in_specs=[vm, vm, hbm, vm, vm, hbm],
        out_specs=vm,
        scratch_shapes=[
            pltpu.VMEM(unembed.shape, BF16),
            pltpu.VMEM(decoder.shape, BF16),
            pltpu.VMEM((2, 2, 2, 4, 16, width), BF16),
            pltpu.VMEM((2, 256, voc_cols), F32),
            pltpu.VMEM((2, 256, voc_cols), BF16),
            pltpu.VMEM((32, 128), F32),
            pltpu.VMEM((1, width), F32),
            pltpu.VMEM((32, slab), F32),
            pltpu.VMEM((1, slab), F32),
            pltpu.VMEM((32, 128), jnp.int32),
            pltpu.VMEM((2, 4, 8, 128), F32),
            pltpu.VMEM((2, 23, 8, 128), F32),
            pltpu.VMEM((2, 8, 2, 2, 4, 2, 16, slab), F32),
            pltpu.VMEM((8, 2, 2, 4, 2, 16, slab), F32),
            pltpu.VMEM((8, 2, 2, 4, 16, slab), BF16),
            pltpu.VMEM((8, 4, 2, 2, 16, slab), BF16),
            pltpu.VMEM((8, 3, 4, 16, slab), BF16),
            pltpu.VMEM((8, 3, 2, 2, 16, slab), BF16),
            pltpu.VMEM((8, 2, 2, 16, slab), BF16),
            pltpu.VMEM((8, 4, 16, slab), BF16),
            pltpu.VMEM((8, 3, 16, slab), BF16),
            pltpu.VMEM((8, 3, 16, slab), BF16),
            pltpu.VMEM((8, 2, 16, slab), F32),
            pltpu.VMEM((2, 7, 16, slab), F32),
            pltpu.VMEM((8, 16, 128), F32),
            pltpu.VMEM((8, 16, 128), F32),
            pltpu.VMEM((8, 32, 128), F32),
            pltpu.VMEM((2, 16, 128), F32),
            pltpu.VMEM((2, 16, 128), F32),
            pltpu.VMEM((2, 32, 128), F32),
            dma((2,)),
            dma((2, 3)), dma((2, 3)),
            dma((2, 4, 2)), dma((2, 4, 2)),
            dma((2, 4)), dma((2, 4)),
            dma((2, 4)), dma((2, 4)),
            dma((2, 23)), dma((2, 23)),
            dma((8,)), dma((8,)),
            dma((8, 3)), dma((8, 3)),
            dma((8, 3)), dma((8, 3)),
            dma((8, 3)), dma((8, 3)),
            dma((8, 3)), dma((8, 3)),
            dma((2, 7)), dma((2, 7)),
            dma((7,)), dma((7,)),
            dma((7,)), dma((7,)),
            dma((7,)), dma((7,)),
            dma((3,)), dma((3,)),
        ],
        compiler_params=pltpu.CompilerParams(
            collective_id=0, has_side_effects=True, vmem_limit_bytes=60 * 1024 * 1024
        ),
    )(resid, norm_gain, unembed, targets.reshape(4, 128), feat_ids, decoder)
    return projected * feat_acts


def solution(mesh):
    placed = (
        P("tok", None),
        P(),
        P(None, ("tok", "voc")),
        P(),
        P("tok", None),
        P("tok", None),
        P("voc", None),
    )
    return jax.shard_map(
        on_device, mesh=mesh, in_specs=placed, out_specs=P("tok", None), check_vma=False
    )
```

```python
import functools

import jax
import jax.numpy as jnp
from jax import lax
from jax.experimental import pallas as pl
from jax.experimental.pallas import tpu as pltpu
from jax.sharding import PartitionSpec as P

EPSILON = 1e-06
MESH = pl.DeviceIdType.MESH
F32 = jnp.float32
BF16 = jnp.bfloat16
CHUNK = 16384
LAG2 = 4
LAG3 = 6


def body(
    resid_ref, gain_ref, unembed_hbm, targets_ref, ids_ref, decoder_hbm,
    out_ref,
    w_ref, dec_ref, nall, ebuf, dirbuf, rms_ref, gain_buf, uslab, gslab, idbuf,
    st_own, st_in, acc, crecv, sx, sy, rx, ry, s2x, s2y, r2x, r2y, zs, zr,
    bz, az, iz, bx, ax, ix,
    load_sem, gy_s, gy_r, gx_s, gx_r, gc_s, gc_r, gd_s, gd_r, st_s, st_r,
    c_s, c_r, x1_s, x1_r, y1_s, y1_r, x2_s, x2_r, y2_s, y2_r, z_s, z_r,
    bz_s, bz_r, az_s, az_r, iz_s, iz_r, fx_s, fx_r,
):
    tok = lax.axis_index("tok")
    voc = lax.axis_index("voc")
    x_lo = tok // 8
    y = (tok // 2) % 4
    core = tok % 2
    x_hi = voc // 8
    z = voc % 8
    x = x_hi * 2 + x_lo

    def device(xx, yy, zz, cc):
        return ((xx % 2) * 8 + yy * 2 + cc, (xx // 2) * 8 + zz)

    def x_peer(k):
        return device((x + k) % 4, y, z, core)

    def y_peer(k):
        return device(x, (y + k) % 4, z, core)

    def z_peer(k):
        return device(x, y, (z + k) % 8, core)

    sibling = device(x, y, z, 1 - core)

    def send(src, dst, s, r, peer):
        return pltpu.make_async_remote_copy(
            src_ref=src, dst_ref=dst, send_sem=s, recv_sem=r, device_id=peer, device_id_type=MESH
        )

    load_w = pltpu.make_async_copy(unembed_hbm, w_ref, load_sem.at[0])
    load_d = pltpu.make_async_copy(decoder_hbm, dec_ref, load_sem.at[1])
    load_w.start()
    load_d.start()
    barrier = pltpu.get_barrier_semaphore()
    peers = [sibling]
    peers += [x_peer(k) for k in (1, 2, 3)]
    peers += [y_peer(k) for k in (1, 2, 3)]
    peers += [z_peer(k) for k in range(1, 8)]
    plane = [(a, b) for a in range(4) for b in range(4) if a + b > 0]
    crossed = [device((x + a) % 4, (y + b) % 4, z, core) for a, b in plane]
    stat_peers = peers[0:1] + crossed + peers[7:14]
    peers = stat_peers
    for peer in peers:
        pl.semaphore_signal(barrier, inc=1, device_id=peer, device_id_type=MESH)

    hidden = resid_ref[...].astype(F32)
    width = hidden.shape[1]
    rms = jnp.sqrt(jnp.mean(hidden * hidden, axis=1, keepdims=True) + EPSILON)
    rms_ref[...] = jnp.broadcast_to(rms, rms_ref.shape)
    gain = gain_ref[...].reshape(1, width)
    gain_buf[...] = gain
    normed = (hidden / rms * gain).astype(BF16)
    for h in range(2):
        nall[h, x_lo, core, y] = normed[h * 16:h * 16 + 16]

    half = width // 2
    slab = half // 8
    pl.semaphore_wait(barrier, len(peers))

    def gy(h, k):
        part = nall.at[h, x_lo, core, y]
        return send(part, part, gy_s.at[h, k - 1], gy_r.at[h, k - 1], y_peer(k))

    def gx(h, kb, d):
        part = nall.at[h, x_lo, core, (y - kb + 4) % 4, :, pl.ds(d * half, half)]
        return send(part, part, gx_s.at[h, kb, d], gx_r.at[h, kb, d], x_peer(1 + 2 * d))

    def gc(h, kb):
        part = nall.at[h, x_lo, core, (y - kb + 4) % 4]
        return send(part, part, gc_s.at[h, kb], gc_r.at[h, kb], sibling)

    def gd(h, kb):
        part = nall.at[h, 1 - x_lo, core, (y - kb + 4) % 4]
        return send(part, part, gd_s.at[h, kb], gd_r.at[h, kb], sibling)

    def pass_on(h, k):
        gy(h, k).wait_recv()
        gx(h, k, 0).start()
        gx(h, k, 1).start()
        gc(h, k).start()

    def pass_over(h, kb):
        gx(h, kb, 0).wait_recv()
        gx(h, kb, 1).wait_recv()
        gd(h, kb).start()

    def gathered(h, own):
        for kb in (0, 1, 3, 2):
            (gc if own else gd)(h, kb).wait_recv()

    for k in (1, 3, 2):
        gy(0, k).start()
    for h in range(2):
        gx(h, 0, 0).start()
        gx(h, 0, 1).start()
    gc(0, 0).start()
    gc(1, 0).start()

    start = pl.multiple_of(x_hi * half, half)
    unit_half = resid_ref[:, pl.ds(start, half)].astype(F32) / rms
    gain_half = gain_buf[:, pl.ds(start, half)]
    for zz in range(8):
        @pl.when(z == zz)
        def _():
            uslab[...] = unit_half[:, zz * slab:(zz + 1) * slab]
            gslab[...] = gain_half[:, zz * slab:(zz + 1) * slab]
    st_own[...] = jnp.zeros_like(st_own)
    idbuf[...] = jnp.zeros_like(idbuf)
    idbuf[:, 0:64] = ids_ref[...]
    low_half = lax.broadcasted_iota(jnp.int32, (16, 128), 1) < 64

    def attribute(values):
        high = values.astype(BF16)
        low = (values - high.astype(F32)).astype(BF16)
        stacked = jnp.concatenate([high, low], axis=0)
        lanes = jnp.bitwise_and(idbuf[...], 127)
        tiles = jnp.right_shift(idbuf[...], 7)

        def step(n, picked):
            cols = pl.ds(pl.multiple_of(n * CHUNK, CHUNK), CHUNK)
            both = jnp.dot(stacked, dec_ref[:, cols], preferred_element_type=F32)
            dots = both[0:32] + both[32:64]
            for q in range(CHUNK // 128):
                got = jnp.take_along_axis(
                    dots[:, q * 128:(q + 1) * 128], lanes, axis=1, mode="promise_in_bounds"
                )
                picked = jnp.where(tiles == n * (CHUNK // 128) + q, got, picked)
            return picked

        picked = lax.fori_loop(0, dec_ref.shape[1] // CHUNK, step, jnp.zeros((32, 128), F32))
        return jnp.where(low_half, picked[0:16], pltpu.roll(picked[16:32], 64, 1))

    def to_voc(buf, s, r):
        return [send(buf.at[z], buf.at[z], s.at[k - 1], r.at[k - 1], z_peer(k)) for k in range(1, 8)]

    load_d.wait()
    bz[z] = attribute(uslab[...])
    for copy in to_voc(bz, bz_s, bz_r):
        copy.start()

    eye = lax.broadcasted_iota(jnp.int32, (128, 128), 0) == lax.broadcasted_iota(jnp.int32, (128, 128), 1)

    def to_row(col):
        return jnp.sum(jnp.where(eye, col, 0.0), axis=0, keepdims=True)

    def to_col(row):
        return jnp.sum(jnp.where(eye, row, 0.0), axis=1, keepdims=True)

    def logits_of(h, xl):
        rows = pl.ds(pl.multiple_of(xl * 128, 128), 128)
        left = nall[h, xl].reshape(128, width)

        def step(n, carry):
            cols = pl.ds(pl.multiple_of(n * 256, 256), 256)
            ebuf[h, rows, cols] = jnp.dot(left, w_ref[:, cols], preferred_element_type=F32)
            return carry

        lax.fori_loop(0, ebuf.shape[2] // 256, step, 0)
        part = ebuf[h, rows]
        top = jnp.max(part, axis=1, keepdims=True)
        part = jnp.exp(part - top)
        ebuf[h, rows] = part
        st_own[h, 0, pl.ds(xl, 1)] = to_row(top)
        st_own[h, 0, pl.ds(2 + xl, 1)] = to_row(jnp.sum(part, axis=1, keepdims=True))

    firsts = [0, 1, 16, 23]

    def st_copies(h, stage):
        return [
            send(st_own.at[h, stage], st_in.at[h, n], st_s.at[h, n], st_r.at[h, n], stat_peers[n])
            for n in range(firsts[stage], firsts[stage + 1])
        ]

    def st_send(h, stage):
        for copy in st_copies(h, stage):
            copy.start()

    def st_merge(h, stage):
        for copy in st_copies(h, stage):
            copy.wait_recv()
        tiles = [st_own[h, stage]] + [st_in[h, n] for n in range(firsts[stage], firsts[stage + 1])]
        merged = functools.reduce(jnp.maximum, [t[0:2] for t in tiles])
        st_own[h, stage + 1, 0:2] = merged
        st_own[h, stage + 1, 2:4] = sum(t[2:4] * jnp.exp(t[0:2] - merged) for t in tiles)
        if stage < 2:
            st_send(h, stage + 1)

    voc_cols = w_ref.shape[1]

    def direction_of(h):
        scale = jnp.exp(st_own[h, 0, 0:2] - st_own[h, 3, 0:2]) / st_own[h, 3, 2:4]
        lane = lax.broadcasted_iota(jnp.int32, (128, voc_cols), 1).astype(F32)
        rel = (targets_ref[...] - (tok * 16 + voc) * voc_cols).astype(F32)
        cols = [to_col(rel[n:n + 1]) for n in range(4)]
        for q in range(2):
            prob = ebuf[h, pl.ds(q * 128, 128)] * to_col(scale[q:q + 1])
            parts = []
            for cc in range(2):
                for yy in range(4):
                    first = (yy % 2) * 64 + cc * 32 + h * 16
                    parts.append(cols[q * 2 + yy // 2][first:first + 16])
            hot = jnp.where(lane == jnp.concatenate(parts, axis=0), 1.0, 0.0)
            dirbuf[h, pl.ds(q * 128, 128)] = (hot - prob).astype(BF16)

    for k in (1, 3, 2):
        gy(1, k).start()
    pass_on(0, 1)
    pass_on(0, 3)
    pass_over(0, 0)
    pass_on(0, 2)
    pass_over(1, 0)
    pass_over(0, 1)
    pass_over(0, 3)
    pass_on(1, 1)
    pass_on(1, 3)
    pass_over(0, 2)
    pass_on(1, 2)
    load_w.wait()
    gathered(0, True)
    logits_of(0, x_lo)
    gathered(0, False)
    logits_of(0, 1 - x_lo)
    st_send(0, 0)
    pass_over(1, 1)
    pass_over(1, 3)
    st_merge(0, 0)
    pass_over(1, 2)
    gathered(1, True)
    logits_of(1, x_lo)
    gathered(1, False)
    logits_of(1, 1 - x_lo)
    st_send(1, 0)
    st_merge(1, 0)
    st_merge(0, 1)

    def cross(buf, n):
        return send(buf.at[0], buf.at[1], fx_s.at[n], fx_r.at[n], x_peer(2))

    def add_voc(buf, s, r, over, n):
        for copy in to_voc(buf, s, r):
            copy.wait_recv()
        over[0] = sum(buf[m] for m in range(8))
        cross(over, n).start()

    add_voc(bz, bz_s, bz_r, bx, 0)
    st_merge(0, 2)
    direction_of(0)

    def c_copy(j):
        return send(acc.at[1 - core, j], crecv.at[j], c_s.at[j], c_r.at[j], sibling)

    def x1(j, k):
        to = (x + k) % 4
        return send(sx.at[j, to // 2, to % 2], rx.at[j, k - 1], x1_s.at[j, k - 1], x1_r.at[j, k - 1], x_peer(k))

    def y1(j, k):
        return send(sy.at[j, (y + k) % 4], ry.at[j, k - 1], y1_s.at[j, k - 1], y1_r.at[j, k - 1], y_peer(k))

    def x2(j, k):
        to = (x + k) % 4
        return send(s2x.at[j, to // 2, to % 2], r2x.at[j, k - 1], x2_s.at[j, k - 1], x2_r.at[j, k - 1], x_peer(k))

    def y2(j, k):
        return send(s2y.at[j, (y + k) % 4], r2y.at[j, k - 1], y2_s.at[j, k - 1], y2_r.at[j, k - 1], y_peer(k))

    def z3(j, sub):
        hop = 2 * (j % 4) + sub
        slot = (j // 4, hop)
        return send(zs.at[j, sub], zr.at[slot], z_s.at[slot], z_r.at[slot], z_peer(hop + 1))

    def multiply(j):
        for sub in range(2):
            group = (z + 1 + 2 * (j % 4) + sub) % 8
            for hx in range(2):
                rows = pl.ds(pl.multiple_of(hx * half + group * slab, 32), slab)
                part = lax.dot_general(
                    dirbuf[j // 4], w_ref[rows, :], (((1,), (1,)), ((), ())), preferred_element_type=F32
                )
                for q in range(4):
                    acc[q % 2, j, hx, q // 2, :, sub] = part[q * 64:(q + 1) * 64].reshape(4, 16, slab)
        c_copy(j).start()

    def first_sum(j):
        c_copy(j).wait_recv()
        for hx in range(2):
            for xl in range(2):
                both = acc[core, j, hx, xl] + crecv[j, hx, xl]
                acc[core, j, hx, xl] = both
                sx[j, hx, xl] = both[:, :, 0:8].reshape(4, 16, slab).astype(BF16)
                for yy in range(4):
                    sy[j, yy, hx, xl] = both[yy, :, 8:16].reshape(16, slab).astype(BF16)
        for k in (2, 1, 3):
            x1(j, k).start()
            y1(j, k).start()

    def second_sum(j):
        for k in (1, 2, 3):
            x1(j, k).wait_recv()
        mine = acc[core, j, x_hi, x_lo, :, :, 0:8].reshape(4, 16, slab)
        for k in range(3):
            mine = mine + rx[j, k].astype(F32)
        acc[core, j, x_hi, x_lo, :, :, 0:8] = mine.reshape(4, 2, 8, slab)
        s2y[j] = mine.astype(BF16)
        for k in (2, 1, 3):
            y2(j, k).start()
        for k in (1, 2, 3):
            y1(j, k).wait_recv()
        other = acc[core, j, :, :, y, :, 8:16].reshape(2, 2, 16, slab)
        for k in range(3):
            other = other + ry[j, k].astype(F32)
        acc[core, j, :, :, y, :, 8:16] = other.reshape(2, 2, 2, 8, slab)
        s2x[j] = other.astype(BF16)
        for k in (2, 1, 3):
            x2(j, k).start()

    def third_sum(j):
        for k in (1, 2, 3):
            y2(j, k).wait_recv()
            x2(j, k).wait_recv()
        upper = acc[core, j, x_hi, x_lo, y, :, 0:8].reshape(16, slab)
        lower = acc[core, j, x_hi, x_lo, y, :, 8:16].reshape(16, slab)
        for k in range(3):
            upper = upper + r2y[j, k].astype(F32)
            lower = lower + r2x[j, k].astype(F32)
        for sub in range(2):
            zs[j, sub, 0:8] = upper[sub * 8:sub * 8 + 8]
            zs[j, sub, 8:16] = lower[sub * 8:sub * 8 + 8]
        z3(j, 0).start()

        @pl.when(j % 4 < 3)
        def _():
            z3(j, 1).start()

    def pipeline(i, carry):
        @pl.when(i == 1)
        def _():
            st_merge(1, 1)

        @pl.when(i == 4)
        def _():
            first_sum(i - 1)
            st_merge(1, 2)
            direction_of(1)

        @pl.when(i < 8)
        def _():
            multiply(i)

        @pl.when((i >= 1) & (i < 9) & (i != 4))
        def _():
            first_sum(i - 1)

        @pl.when((i >= LAG2) & (i < 8 + LAG2))
        def _():
            second_sum(i - LAG2)

        @pl.when(i >= LAG3)
        def _():
            third_sum(i - LAG3)

        return carry

    lax.fori_loop(0, 8 + LAG3, pipeline, 0)
    grads = []
    for h in range(2):
        total = zs[h * 4 + 3, 1]
        for hop in range(7):
            z3(h * 4 + hop // 2, hop % 2).wait_recv()
            total = total + zr[h, hop]
        grads.append(total)
    grad = jnp.concatenate(grads, axis=0)

    scaled = grad * gslab[...]
    inner = jnp.sum(uslab[...] * scaled, axis=1, keepdims=True)
    iz[z] = jnp.broadcast_to(inner, (32, 128))
    for copy in to_voc(iz, iz_s, iz_r):
        copy.start()
    az[z] = attribute(scaled)
    for copy in to_voc(az, az_s, az_r):
        copy.start()
    add_voc(iz, iz_s, iz_r, ix, 1)
    for h in range(2):
        for k in (1, 2, 3):
            gy(h, k).wait_send()
        for kb in range(4):
            gx(h, kb, 0).wait_send()
            gx(h, kb, 1).wait_send()
            gc(h, kb).wait_send()
            gd(h, kb).wait_send()
        for stage in range(3):
            for copy in st_copies(h, stage):
                copy.wait_send()

    def drain(j, carry):
        c_copy(j).wait_send()
        for k in (1, 2, 3):
            x1(j, k).wait_send()
            y1(j, k).wait_send()
            x2(j, k).wait_send()
            y2(j, k).wait_send()

        z3(j, 0).wait_send()

        @pl.when(j % 4 < 3)
        def _():
            z3(j, 1).wait_send()

        return carry

    lax.fori_loop(0, 8, drain, 0)
    add_voc(az, az_s, az_r, ax, 2)
    cross(bx, 0).wait_recv()
    cross(ix, 1).wait_recv()
    unit_dot = bx[0] + bx[1]
    mean = (ix[0] + ix[1]) * (1.0 / width)
    scale = 1.0 / rms_ref[...]
    cross(ax, 2).wait_recv()
    both = ax[0] + ax[1]
    for n in range(2):
        rows = slice(n * 16, n * 16 + 16)
        if n == 1:
            both = pltpu.roll(both, 64, 1)
            unit_dot = pltpu.roll(unit_dot, 64, 1)
        out_ref[rows] = ((both - unit_dot * mean[rows]) * scale[rows])[:, 0:64]

    for copy in to_voc(bz, bz_s, bz_r) + to_voc(az, az_s, az_r) + to_voc(iz, iz_s, iz_r):
        copy.wait_send()
    for n, over in enumerate((bx, ix, ax)):
        cross(over, n).wait_send()


def on_device(resid, norm_gain, unembed, targets, feat_ids, feat_acts, decoder):
    width = resid.shape[1]
    voc_cols = unembed.shape[1]
    slab, features = decoder.shape
    vm = pl.BlockSpec(memory_space=pltpu.VMEM)
    hbm = pl.BlockSpec(memory_space=pl.ANY)
    dma = pltpu.SemaphoreType.DMA
    projected = pl.pallas_call(
        body,
        out_shape=jax.ShapeDtypeStruct(feat_acts.shape, F32),
        in_specs=[vm, vm, hbm, vm, vm, hbm],
        out_specs=vm,
        scratch_shapes=[
            pltpu.VMEM(unembed.shape, BF16),
            pltpu.VMEM(decoder.shape, BF16),
            pltpu.VMEM((2, 2, 2, 4, 16, width), BF16),
            pltpu.VMEM((2, 256, voc_cols), F32),
            pltpu.VMEM((2, 256, voc_cols), BF16),
            pltpu.VMEM((32, 128), F32),
            pltpu.VMEM((1, width), F32),
            pltpu.VMEM((32, slab), F32),
            pltpu.VMEM((1, slab), F32),
            pltpu.VMEM((32, 128), jnp.int32),
            pltpu.VMEM((2, 4, 8, 128), F32),
            pltpu.VMEM((2, 23, 8, 128), F32),
            pltpu.VMEM((2, 8, 2, 2, 4, 2, 16, slab), F32),
            pltpu.VMEM((8, 2, 2, 4, 2, 16, slab), F32),
            pltpu.VMEM((8, 2, 2, 4, 16, slab), BF16),
            pltpu.VMEM((8, 4, 2, 2, 16, slab), BF16),
            pltpu.VMEM((8, 3, 4, 16, slab), BF16),
            pltpu.VMEM((8, 3, 2, 2, 16, slab), BF16),
            pltpu.VMEM((8, 2, 2, 16, slab), BF16),
            pltpu.VMEM((8, 4, 16, slab), BF16),
            pltpu.VMEM((8, 3, 16, slab), BF16),
            pltpu.VMEM((8, 3, 16, slab), BF16),
            pltpu.VMEM((8, 2, 16, slab), F32),
            pltpu.VMEM((2, 7, 16, slab), F32),
            pltpu.VMEM((8, 16, 128), F32),
            pltpu.VMEM((8, 16, 128), F32),
            pltpu.VMEM((8, 32, 128), F32),
            pltpu.VMEM((2, 16, 128), F32),
            pltpu.VMEM((2, 16, 128), F32),
            pltpu.VMEM((2, 32, 128), F32),
            dma((2,)),
            dma((2, 3)), dma((2, 3)),
            dma((2, 4, 2)), dma((2, 4, 2)),
            dma((2, 4)), dma((2, 4)),
            dma((2, 4)), dma((2, 4)),
            dma((2, 23)), dma((2, 23)),
            dma((8,)), dma((8,)),
            dma((8, 3)), dma((8, 3)),
            dma((8, 3)), dma((8, 3)),
            dma((8, 3)), dma((8, 3)),
            dma((8, 3)), dma((8, 3)),
            dma((2, 7)), dma((2, 7)),
            dma((7,)), dma((7,)),
            dma((7,)), dma((7,)),
            dma((7,)), dma((7,)),
            dma((3,)), dma((3,)),
        ],
        compiler_params=pltpu.CompilerParams(
            collective_id=0, has_side_effects=True, vmem_limit_bytes=60 * 1024 * 1024
        ),
    )(resid, norm_gain, unembed, targets.reshape(4, 128), feat_ids, decoder)
    return projected * feat_acts


def solution(mesh):
    placed = (
        P("tok", None),
        P(),
        P(None, ("tok", "voc")),
        P(),
        P("tok", None),
        P("tok", None),
        P("voc", None),
    )
    return jax.shard_map(
        on_device, mesh=mesh, in_specs=placed, out_specs=P("tok", None), check_vma=False
    )
```
